256 devices in a mesh: grp: 16 (over z_lo, x), dev: 16 (over y, z_hi, core).
Axes of the slice: x: 4, y: 4, z: 8 (z_hi: 2, z_lo: 4; z = z_hi * 4 + z_lo), core: 2. Of those that a mesh axis runs over, the one named last changes fastest.
Arguments:
- teacher_image: bfloat16 [16384, 1280], P(('grp', 'dev')), may hold values from -4 to 4
- teacher_text: bfloat16 [16384, 1280], P(('grp', 'dev')), may hold values from -4 to 4
- student_image: bfloat16 [16384, 512], P(('grp', 'dev')), may hold values from -4 to 4
- student_text: bfloat16 [16384, 512], P(('grp', 'dev')), may hold values from -4 to 4
- teacher_scale: float32 [1], replicated, may hold values from 2 to 4
- student_scale: float32 [1], replicated, may hold values from 2 to 4
Outputs:
- grad_image: float32 [16384, 512], P(('grp', 'dev'))
- grad_text: float32 [16384, 512], P(('grp', 'dev'))
- loss: float32 [1], replicated
- grad_scale: float32 [1], replicated
The draws below stay inside these ranges and needn't reach their ends.
All inputs are finite; a program needn't handle non-finite values.
Results may differ from the reference program's by a relative error of at most 0.0028.
Values may be sent and summed in bfloat16 or wider, within the bound.
A program may use at most 64 MiB of HBM per device.

```python
import math
import jax
import jax.numpy as jnp
from jax import lax

TEACH_W = 1280
STUD_W = 512
PAIRS = 16384


def drawn_rows(key, width, lower, upper):
    values = jnp.clip(jax.random.normal(jax.random.fold_in(key, 7), (PAIRS, width), jnp.float32), -4.0, 4.0)
    spread = jax.random.uniform(jax.random.fold_in(key, 8), (PAIRS, 1), jnp.float32, jnp.log(lower), jnp.log(upper))
    return values * width ** (-0.25) * jnp.exp(spread)


def image_rows(key, width, align, lower, upper):
    base = drawn_rows(key, width, lower, upper)
    index = jnp.arange(PAIRS, dtype=jnp.int32)
    chosen = (index % 64 == 3).astype(jnp.float32)[:, None] * align
    return base * (1.0 - chosen)


def text_rows(key, width, align, lower, upper):
    base = drawn_rows(key, width, lower, upper)
    index = jnp.arange(PAIRS, dtype=jnp.int32)
    half = PAIRS // 2
    source_one = (index - half) % PAIRS
    chosen_one = (source_one % 64 == 3).astype(jnp.float32)[:, None] * align
    rest = 1.0 - chosen_one
    return base * rest


def draw_teacher_image(key, part):
    key = jax.random.fold_in(key, 1)
    return image_rows(key, TEACH_W, 0.0, 1.0, 1.0).astype(jnp.bfloat16)


def draw_teacher_text(key, part):
    key = jax.random.fold_in(key, 2)
    return text_rows(key, TEACH_W, 0.0, 1.0, 1.0).astype(jnp.bfloat16)


def draw_student_image(key, part):
    key = jax.random.fold_in(key, 3)
    return image_rows(key, STUD_W, 0.0, 1.0, 1.0).astype(jnp.bfloat16)


def draw_student_text(key, part):
    key = jax.random.fold_in(key, 4)
    return text_rows(key, STUD_W, 0.0, 1.0, 1.0).astype(jnp.bfloat16)


def setup_inputs(seed: int = 0) -> dict:
    streams_of = jax.random.split(jax.random.key(seed), 7)
    return {
        "teacher_image": draw_teacher_image(jax.random.fold_in(streams_of[6], 71), 0),
        "teacher_text": draw_teacher_text(jax.random.fold_in(streams_of[6], 71), 0),
        "student_image": draw_student_image(jax.random.fold_in(streams_of[6], 71), 0),
        "student_text": draw_student_text(jax.random.fold_in(streams_of[6], 71), 0),
        "teacher_scale": jnp.clip(jnp.exp(jax.random.uniform(streams_of[4], (1,), jnp.float32, math.log(2.0), math.log(4.0))), 2.0, 4.0),
        "student_scale": jnp.clip(jnp.exp(jax.random.uniform(streams_of[5], (1,), jnp.float32, math.log(2.0), math.log(4.0))), 2.0, 4.0),
    }


def reference(teacher_image, teacher_text, student_image, student_text, teacher_scale, student_scale):
    teach_scale = teacher_scale[0]
    learn_scale = student_scale[0]
    block = math.gcd(PAIRS, 512)
    count = PAIRS // block
    starts = jnp.arange(count, dtype=jnp.int32) * block

    def logits(start):
        picked_image = lax.dynamic_slice_in_dim(teacher_image, start, block, 0)
        picked_learn = lax.dynamic_slice_in_dim(student_image, start, block, 0)
        teacher = teach_scale * jnp.dot(picked_image, teacher_text.T, preferred_element_type=jnp.float32)
        student = learn_scale * jnp.dot(picked_learn, student_text.T, preferred_element_type=jnp.float32)
        return teacher, student, picked_learn

    def row_lse(values):
        peak = jnp.max(values, axis=1)
        return peak + jnp.log(jnp.sum(jnp.exp(values - peak[:, None]), axis=1))

    def column_update(peak, total, values):
        newer = jnp.maximum(peak, jnp.max(values, axis=0))
        total = total * jnp.exp(peak - newer) + jnp.sum(jnp.exp(values - newer[None, :]), axis=0)
        return newer, total

    def first_pass(carry, start):
        tpeak, ttotal, speak, stotal = carry
        teacher, student, unused = logits(start)
        tpeak, ttotal = column_update(tpeak, ttotal, teacher)
        speak, stotal = column_update(speak, stotal, student)
        return (tpeak, ttotal, speak, stotal), (row_lse(teacher), row_lse(student))

    lowest = jnp.full((PAIRS,), -jnp.inf, jnp.float32)
    zeros = jnp.zeros((PAIRS,), jnp.float32)
    carry, rows_out = lax.scan(first_pass, (lowest, zeros, lowest, zeros), starts)
    col_teach = carry[0] + jnp.log(carry[1])
    col_stud = carry[2] + jnp.log(carry[3])
    row_teach = rows_out[0].reshape(PAIRS)
    row_stud = rows_out[1].reshape(PAIRS)

    def second_pass(carry, inputs):
        text_acc, loss_acc, scale_acc = carry
        start, teach_lse, stud_lse = inputs
        teacher, student, picked_learn = logits(start)
        p_teach = jnp.exp(teacher - teach_lse[:, None])
        q_teach = jnp.exp(teacher - col_teach[None, :])
        p_stud = jnp.exp(student - stud_lse[:, None])
        q_stud = jnp.exp(student - col_stud[None, :])
        differ = p_stud + q_stud - p_teach - q_teach
        loss_acc = loss_acc - jnp.sum((p_teach + q_teach) * student)
        scale_acc = scale_acc + jnp.sum(differ * student)
        weights = (0.5 * learn_scale * differ).astype(jnp.bfloat16)
        image_grad = jnp.dot(weights, student_text, preferred_element_type=jnp.float32)
        text_acc = text_acc + jnp.dot(weights.T, picked_learn, preferred_element_type=jnp.float32)
        return (text_acc, loss_acc, scale_acc), image_grad

    init = (jnp.zeros((PAIRS, STUD_W), jnp.float32), jnp.zeros((), jnp.float32), jnp.zeros((), jnp.float32))
    carry, image_blocks = lax.scan(second_pass, init, (starts, rows_out[0], rows_out[1]))
    grad_image = image_blocks.reshape(PAIRS, STUD_W)
    grad_text = carry[0]
    loss = (jnp.sum(row_stud) + jnp.sum(col_stud) + carry[1]) / (2.0 * PAIRS)
    grad_scale = carry[2] / (2.0 * PAIRS * learn_scale)
    return grad_image, grad_text, loss.reshape(1), grad_scale.reshape(1)
```

```python
import functools

import jax
import jax.numpy as jnp
from jax import lax
from jax.experimental import pallas as pl
from jax.experimental.pallas import tpu as pltpu
from jax.sharding import PartitionSpec as P

NX, NY, NZ = 4, 4, 8
ROWS = 64
TW, SW = 1280, 512
W = TW + SW
TILE = 1024
CHUNK = 256
SUB = 64
LOG2E = 1.4426950408889634
LN2 = 0.6931471805599453
MESH = pl.DeviceIdType.MESH
NT = (((1,), (1,)), ((), ()))
TN = (((0,), (0,)), ((), ()))


def kernel(
    ti, tt, si, st, tscale, sscale,
    gi_out, gt_out, loss_out, gs_out,
    img, txt, dtmp, ert, ect, ers, ecs, ds, wts,
    mrow, arow, lrow, cmax, csum, bcol,
    rst, cst, rst_in, cst_in,
    gi_own, gi_snd, gi_in, gt_all, gt_sib, gt_own, gt_snd, gt_in,
    sc_snd, sc_a, sc_mid, sc_b,
    loc_sem, ps_s, ps_r, zs_s, zs_r, cs_s, cs_r,
    rx_s, rx_r, cx_s, cx_r, gi_s, gi_r, sb_s, sb_r, gt_s, gt_r,
    sa_s, sa_r, sb2_s, sb2_r,
):
    g, d = lax.axis_index("grp"), lax.axis_index("dev")
    x, y, z, c = g % 4, d // 4, ((d // 2) % 2) * 4 + g // 4, d % 2
    me_p, me_c = y * 4 + x, z * 2 + c
    sib = 1 - c

    def at(xx, yy, zz, cc):
        return ((zz % 4) * 4 + xx, yy * 4 + (zz // 4) * 2 + cc)

    plane = [(dx, dy) for dy in range(NY) for dx in range(NX) if (dx, dy) != (0, 0)]
    column = [(dz, dc) for dz in range(NZ) for dc in range(2) if (dz, dc) != (0, 0)]

    def plane_peer(dx, dy):
        px, py = (x + dx) % NX, (y + dy) % NY
        return py * 4 + px, at(px, py, z, c)

    def column_peer(dz, dc):
        pz, pc = (z + dz) % NZ, (c + dc) % 2
        return pz * 2 + pc, at(x, y, pz, pc)

    local = []
    for k, (src, dst) in enumerate((
        (ti, img.at[y, x, :, pl.ds(0, TW)]),
        (si, img.at[y, x, :, pl.ds(TW, SW)]),
        (tt, txt.at[z, c, :, pl.ds(0, TW)]),
        (st, txt.at[z, c, :, pl.ds(TW, SW)]),
    )):
        cp = pltpu.make_async_copy(src, dst, loc_sem.at[k])
        cp.start()
        local.append(cp)

    barrier = pltpu.get_barrier_semaphore()
    for dx, dy in plane:
        pl.semaphore_signal(barrier, inc=1, device_id=plane_peer(dx, dy)[1], device_id_type=MESH)
    for dz, dc in column:
        pl.semaphore_signal(barrier, inc=1, device_id=column_peer(dz, dc)[1], device_id_type=MESH)
    for cp in local:
        cp.wait()
    pl.semaphore_wait(barrier, len(plane) + len(column))

    sent = []

    def send(src, dst, ssem, rsem, dev):
        cp = pltpu.make_async_remote_copy(
            src_ref=src, dst_ref=dst, send_sem=ssem, recv_sem=rsem, device_id=dev, device_id_type=MESH
        )
        cp.start()
        sent.append(cp)

    def arrived(dst, ssem, rsem, dev):
        pltpu.make_async_remote_copy(
            src_ref=dst, dst_ref=dst, send_sem=ssem, recv_sem=rsem, device_id=dev, device_id_type=MESH
        ).wait_recv()

    first, second = (x, y), (y, x)

    def region(h, a, b, r0, n):
        return img.at[b if h == 0 else a, a if h == 0 else b, pl.ds(32 * h + r0, n)]

    def chip(h, a, b):
        return at(a, b, z, c) if h == 0 else at(b, a, z, c)

    def sem_id(h, stage, sign, k):
        return 20 * h + (0, 2, 4, 12)[stage] + (sign > 0) + 2 * k

    def psend(h, stage, sign, k, reg, dev):
        i = sem_id(h, stage, sign, k)
        send(reg, reg, ps_s.at[i], ps_r.at[i], dev)

    def pwait(h, stage, sign, k, reg, dev):
        i = sem_id(h, stage, sign, k)
        arrived(reg, ps_s.at[i], ps_r.at[i], dev)

    def step(v, s, n):
        return (v + s + n) % n

    def a_of(h, k):
        return step(first[h], (0, -1, 1, 2)[k], 4)

    def t1_send(h, k):
        a, b = a_of(h, k), second[h]
        for sign in (1, -1):
            psend(h, 2, sign, k, region(h, a, b, 0, 32), chip(h, first[h], step(b, sign, 4)))

    def t1_recv(h, k):
        a, b = a_of(h, k), second[h]
        for sign in (1, -1):
            src = step(b, -sign, 4)
            pwait(h, 2, sign, k, region(h, a, src, 0, 32), chip(h, first[h], src))
            psend(h, 3, sign, k, region(h, a, src, 0 if sign > 0 else 16, 16), chip(h, first[h], step(b, sign, 4)))

    def t2_recv(h, k):
        a, b = a_of(h, k), second[h]
        for sign in (1, -1):
            pwait(h, 3, sign, k, region(h, a, step(b, 2, 4), 0 if sign > 0 else 16, 16), chip(h, first[h], step(b, -sign, 4)))

    def z_send(sign, s):
        zz = step(z, -sign * (s - 1), 8)
        reg = txt.at[zz, c] if s < 4 else txt.at[zz, c, pl.ds(0 if sign > 0 else 32, 32)]
        i = (s - 1) * 2 + (sign > 0)
        send(reg, reg, zs_s.at[i], zs_r.at[i], at(x, y, step(z, sign, 8), c))

    def z_recv(sign, s):
        zz = step(z, -sign * s, 8)
        reg = txt.at[zz, c] if s < 4 else txt.at[zz, c, pl.ds(0 if sign > 0 else 32, 32)]
        i = (s - 1) * 2 + (sign > 0)
        arrived(reg, zs_s.at[i], zs_r.at[i], at(x, y, step(z, -sign, 8), c))

    def c_send(dz):
        zz = step(z, dz, 8)
        send(txt.at[zz, c], txt.at[zz, c], cs_s.at[dz % 8], cs_r.at[dz % 8], at(x, y, z, sib))

    def c_recv(dz):
        zz = step(z, dz, 8)
        arrived(txt.at[zz, sib], cs_s.at[dz % 8], cs_r.at[dz % 8], at(x, y, z, sib))

    for h in (0, 1):
        for sign in (1, -1):
            psend(h, 0, sign, 0, region(h, first[h], second[h], 0, 32), chip(h, step(first[h], sign, 4), second[h]))
    for sign in (1, -1):
        z_send(sign, 1)
    c_send(0)
    for h in (0, 1):
        t1_send(h, 0)
    for h in (0, 1):
        for k, sign in ((1, 1), (2, -1)):
            src = step(first[h], -sign, 4)
            pwait(h, 0, sign, 0, region(h, src, second[h], 0, 32), chip(h, src, second[h]))
            psend(h, 1, sign, 0, region(h, src, second[h], 0 if sign > 0 else 16, 16), chip(h, step(first[h], sign, 4), second[h]))
            t1_send(h, k)
    for sign in (1, -1):
        z_recv(sign, 1)
        z_send(sign, 2)
        c_send(-sign)
    for h in (0, 1):
        t1_recv(h, 0)
    for h in (0, 1):
        for sign in (1, -1):
            pwait(h, 1, sign, 0, region(h, step(first[h], 2, 4), second[h], 0 if sign > 0 else 16, 16), chip(h, step(first[h], -sign, 4), second[h]))
        t1_send(h, 3)
    for h in (0, 1):
        t1_recv(h, 1)
    for sign in (1, -1):
        z_recv(sign, 2)
        z_send(sign, 3)
        c_send(-2 * sign)
    for h in (0, 1):
        t1_recv(h, 2)
    for h in (0, 1):
        t1_recv(h, 3)
    for sign in (1, -1):
        z_recv(sign, 3)
        z_send(sign, 4)
        c_send(-3 * sign)
    for h in (0, 1):
        for k in range(4):
            t2_recv(h, k)
    for sign in (1, -1):
        z_recv(sign, 4)
    c_send(4)
    for dz in range(8):
        c_recv(dz)

    lt, ls = tscale[0] * LOG2E, sscale[0] * LOG2E

    def fold(v, op):
        return op(v.reshape(v.shape[0] // 8, 8, v.shape[1]), axis=0)

    def pass1(q, carry):
        for part, (lo, hi, scale, er, ec) in enumerate(((0, TW, lt, ert, ect), (TW, W, ls, ers, ecs))):
            left = img[q, :, :, lo:hi].reshape(CHUNK, hi - lo)
            right = txt[:, :, :, lo:hi].reshape(TILE, hi - lo)
            base = 0 if part == 0 else q * CHUNK
            raw = dtmp if part == 0 else ds
            raw[pl.ds(base, CHUNK), :] = lax.dot_general(left, right, NT, preferred_element_type=jnp.float32)

            def by_row(s, peak):
                rows = pl.ds(q * CHUNK + s * SUB, SUB)
                v = raw[pl.ds(base + s * SUB, SUB), :]
                m = jnp.max(v, axis=1, keepdims=True)
                e = jnp.exp2((v - m) * scale)
                er[rows, :] = e
                mrow[part, rows, :] = m * scale
                lrow[part, rows, :] = m * scale + jnp.log2(jnp.sum(e, axis=1, keepdims=True))
                return jnp.maximum(peak, fold(v, jnp.max))

            peak = lax.fori_loop(0, CHUNK // SUB, by_row, jnp.full((8, TILE), -jnp.inf, jnp.float32))
            peak = jnp.max(peak, axis=0, keepdims=True)

            def by_col(s, total):
                rows = pl.ds(q * CHUNK + s * SUB, SUB)
                e = jnp.exp2((raw[pl.ds(base + s * SUB, SUB), :] - peak) * scale)
                ec[rows, :] = e
                return total + fold(e, jnp.sum)

            total = lax.fori_loop(0, CHUNK // SUB, by_col, jnp.zeros((8, TILE), jnp.float32))
            cmax[part, q] = peak * scale
            csum[part, q] = jnp.sum(total, axis=0, keepdims=True)
        return carry

    lax.fori_loop(0, TILE // CHUNK, pass1, 0)

    eye = lax.broadcasted_iota(jnp.int32, (128, 128), 0) == lax.broadcasted_iota(jnp.int32, (128, 128), 1)
    for part in range(2):
        m = jnp.max(cmax[part], axis=0)
        total = jnp.sum(csum[part] * jnp.exp2(cmax[part] - m[None]), axis=0)
        lse = m + jnp.log2(total)
        for k in range(8):
            cst[pl.ds(part * 8 + k, 1), :] = lse[:, 128 * k:128 * k + 128]
    for dz, dc in column:
        i, dev = column_peer(dz, dc)
        send(cst, cst_in.at[me_c], cx_s.at[i], cx_r.at[me_c], dev)
    for part in range(2):
        for k in range(8):
            v = lrow[part, pl.ds(128 * k, 128), :]
            rst[pl.ds(part * 8 + k, 1), :] = jnp.sum(jnp.where(eye, v, 0.0), axis=0, keepdims=True)
    for dx, dy in plane:
        i, dev = plane_peer(dx, dy)
        send(rst, rst_in.at[me_p], rx_s.at[i], rx_r.at[me_p], dev)
    cst_in[me_c] = cst[...]
    rst_in[me_p] = rst[...]

    def total_lse(v):
        m = jnp.max(v, axis=0)
        return m + jnp.log2(jnp.sum(jnp.exp2(v - m[None]), axis=0))

    half = 0.5 * sscale[0]
    for dz, dc in column:
        i, dev = column_peer(dz, dc)
        arrived(cst_in.at[i], cx_s.at[i], cx_r.at[i], dev)
    col = total_lse(cst_in[...])
    for part in range(2):
        lse = jnp.concatenate([col[part * 8 + k:part * 8 + k + 1, :] for k in range(8)], axis=1)
        bcol[part] = half * jnp.exp2(cmax[part] - lse[None])
    for dx, dy in plane:
        i, dev = plane_peer(dx, dy)
        arrived(rst_in.at[i], rx_s.at[i], rx_r.at[i], dev)
    row = total_lse(rst_in[...])
    for part in range(2):
        for k in range(8):
            v = jnp.broadcast_to(row[part * 8 + k:part * 8 + k + 1, :], (128, 128))
            lse = jnp.sum(jnp.where(eye, v, 0.0), axis=1, keepdims=True)
            rows = pl.ds(128 * k, 128)
            arow[part, rows, :] = half * jnp.exp2(mrow[part, rows, :] - lse)

    def pass2(s, carry):
        loss_acc, scale_acc = carry
        rows = pl.ds(s * SUB, SUB)
        q = s // (CHUNK // SUB)
        v = ds[rows, :]
        teach = ert[rows, :] * arow[0, rows, :] + ect[rows, :] * bcol[0, q]
        stud = ers[rows, :] * arow[1, rows, :] + ecs[rows, :] * bcol[1, q]
        differ = stud - teach
        wts[rows, :] = differ.astype(jnp.bfloat16)
        return loss_acc + fold(teach * v, jnp.sum), scale_acc + fold(differ * v, jnp.sum)

    zero = jnp.zeros((8, TILE), jnp.float32)
    loss_acc, scale_acc = lax.fori_loop(0, TILE // SUB, pass2, (zero, zero))

    def narrow(v):
        return functools.reduce(jnp.add, [v[:, 128 * k:128 * k + 128] for k in range(8)])

    sc_snd[pl.ds(0, 8), :] = (row[8:, :] + col[8:, :]) * (LN2 / 16.0) - 2.0 * narrow(loss_acc)
    sc_snd[pl.ds(8, 8), :] = 2.0 * narrow(scale_acc)
    for dx, dy in plane:
        i, dev = plane_peer(dx, dy)
        send(sc_snd, sc_a.at[me_p], sa_s.at[i], sa_r.at[me_p], dev)

    for q in range(4):
        v = lax.dot_general(
            wts[:, 256 * q:256 * q + 256], img[:, :, :, TW:].reshape(TILE, SW), TN, preferred_element_type=jnp.float32
        )
        gt_all[pl.ds(2 * q, 2)] = v.reshape(2, 2, ROWS, SW)
    send(gt_all.at[:, sib], gt_sib, sb_s, sb_r, at(x, y, z, sib))

    for q in range(4):
        v = jnp.dot(
            wts[pl.ds(256 * q, 256), :], txt[:, :, :, TW:].reshape(TILE, SW), preferred_element_type=jnp.float32
        )
        gi_own[pl.ds(4 * q, 4)] = v.reshape(4, ROWS, SW)
        gi_snd[pl.ds(4 * q, 4)] = v.reshape(4, ROWS, SW).astype(jnp.bfloat16)
    for dx, dy in plane:
        i, dev = plane_peer(dx, dy)
        send(gi_snd.at[i], gi_in.at[me_p], gi_s.at[i], gi_r.at[me_p], dev)

    arrived(gt_sib, sb_s, sb_r, at(x, y, z, sib))
    for q in range(8):
        v = gt_all[q, c] + gt_sib[q]
        gt_own[q] = v
        gt_snd[q] = v.astype(jnp.bfloat16)
    for dz in range(1, 8):
        pz = (z + dz) % 8
        send(gt_snd.at[pz], gt_in.at[z], gt_s.at[pz], gt_r.at[z], at(x, y, pz, c))

    v = sc_snd[...]
    for dx, dy in plane:
        i, dev = plane_peer(dx, dy)
        arrived(sc_a.at[i], sa_s.at[i], sa_r.at[i], dev)
    sc_a[me_p] = v
    sc_mid[...] = jnp.sum(sc_a[...], axis=0)
    for dz, dc in column:
        i, dev = column_peer(dz, dc)
        send(sc_mid, sc_b.at[me_c], sb2_s.at[i], sb2_r.at[me_c], dev)

    gi_out[...] = gi_own[me_p]
    for dx, dy in plane:
        i, dev = plane_peer(dx, dy)
        arrived(gi_in.at[i], gi_s.at[i], gi_r.at[i], dev)
        gi_out[...] += gi_in[i].astype(jnp.float32)
    gt_out[...] = gt_own[z]
    for dz in range(1, 8):
        pz = (z + dz) % 8
        arrived(gt_in.at[pz], gt_s.at[pz], gt_r.at[pz], at(x, y, pz, c))
        gt_out[...] += gt_in[pz].astype(jnp.float32)
    for dz, dc in column:
        i, dev = column_peer(dz, dc)
        arrived(sc_b.at[i], sb2_s.at[i], sb2_r.at[i], dev)
    sc_b[me_c] = sc_mid[...]
    total = jnp.sum(sc_b[...], axis=0)
    pairs = 2.0 * TILE * 16
    loss_out[0] = jnp.sum(total[:8]) / pairs
    gs_out[0] = jnp.sum(total[8:]) / (pairs * sscale[0])
    for cp in sent:
        cp.wait_send()


def shards(*args):
    f32, bf16 = jnp.float32, jnp.bfloat16
    anyw = pl.BlockSpec(memory_space=pl.ANY)
    vmem = pl.BlockSpec(memory_space=pltpu.VMEM)
    smem = pl.BlockSpec(memory_space=pltpu.SMEM)
    sem = pltpu.SemaphoreType.DMA
    V = pltpu.VMEM
    return tuple(pl.pallas_call(
        kernel,
        out_shape=(
            jax.ShapeDtypeStruct((ROWS, SW), f32),
            jax.ShapeDtypeStruct((ROWS, SW), f32),
            jax.ShapeDtypeStruct((1,), f32),
            jax.ShapeDtypeStruct((1,), f32),
        ),
        in_specs=[anyw] * 4 + [smem] * 2,
        out_specs=(vmem, vmem, smem, smem),
        scratch_shapes=[
            V((NY, NX, ROWS, W), bf16),
            V((NZ, 2, ROWS, W), bf16),
            V((CHUNK, TILE), f32),
            V((TILE, TILE), f32),
            V((TILE, TILE), f32),
            V((TILE, TILE), f32),
            V((TILE, TILE), f32),
            V((TILE, TILE), f32),
            V((TILE, TILE), bf16),
            V((2, TILE, 1), f32),
            V((2, TILE, 1), f32),
            V((2, TILE, 1), f32),
            V((2, 4, 1, TILE), f32),
            V((2, 4, 1, TILE), f32),
            V((2, 4, 1, TILE), f32),
            V((16, 128), f32),
            V((16, 128), f32),
            V((16, 16, 128), f32),
            V((16, 16, 128), f32),
            V((16, ROWS, SW), f32),
            V((16, ROWS, SW), bf16),
            V((16, ROWS, SW), bf16),
            V((8, 2, ROWS, SW), f32),
            V((8, ROWS, SW), f32),
            V((8, ROWS, SW), f32),
            V((8, ROWS, SW), bf16),
            V((8, ROWS, SW), bf16),
            V((16, 128), f32),
            V((16, 16, 128), f32),
            V((16, 128), f32),
            V((16, 16, 128), f32),
            sem((4,)),
            sem((40,)), sem((40,)),
            sem((8,)), sem((8,)),
            sem((8,)), sem((8,)),
            sem((16,)), sem((16,)),
            sem((16,)), sem((16,)),
            sem((16,)), sem((16,)),
            sem, sem,
            sem((8,)), sem((8,)),
            sem((16,)), sem((16,)),
            sem((16,)), sem((16,)),
        ],
        compiler_params=pltpu.CompilerParams(
            collective_id=0, has_side_effects=True, vmem_limit_bytes=60 * 1024 * 1024
        ),
    )(*args))


def solution(mesh):
    return jax.shard_map(
        shards,
        mesh=mesh,
        in_specs=(
            P(("grp", "dev"), None),
            P(("grp", "dev"), None),
            P(("grp", "dev"), None),
            P(("grp", "dev"), None),
            P(),
            P(),
        ),
        out_specs=(P(("grp", "dev"), None), P(("grp", "dev"), None), P(), P()),
        check_vma=False,
    )
```

```python
import functools

import jax
import jax.numpy as jnp
from jax import lax
from jax.experimental import pallas as pl
from jax.experimental.pallas import tpu as pltpu
from jax.sharding import PartitionSpec as P

NX, NY, NZ = 4, 4, 8
ROWS = 64
TW, SW = 1280, 512
W = TW + SW
TILE = 1024
CHUNK = 256
LOG2E = 1.4426950408889634
LN2 = 0.6931471805599453
MESH = pl.DeviceIdType.MESH
NT = (((1,), (1,)), ((), ()))
TN = (((0,), (0,)), ((), ()))

A_OF = (0, 3, 1, 2)
SLOT = (0, 1, 3, 5, 7, 6, 4, 2)
STRIPS = ((0, 512), (512, 256), (768, 256))
LAST = ((0, 512), (512, 512))


def row_unit(h, a, b):
    k = A_OF.index(a)
    if b == 0:
        return 128 * h + 32 * a
    if b == 2:
        return 768 + 64 * k + 32 * h
    return 256 + 128 * k + (0 if b == 3 else 64) + 32 * h


UNITS = tuple((h, a, b, row_unit(h, a, b)) for h in range(2) for a in range(4) for b in range(4))


def lanes(v, op):
    return functools.reduce(op, [v[:, 128 * k:128 * k + 128] for k in range(v.shape[1] // 128)])


def sublanes(v, op):
    return functools.reduce(op, [v[8 * k:8 * k + 8] for k in range(v.shape[0] // 8)])


def wide(v, n):
    return jnp.concatenate([v] * n, axis=1)


def tall(v, n):
    return jnp.concatenate([v] * n, axis=0)


def kernel(
    ti, tt, si, st, tscale, sscale,
    gi_out, gt_out, loss_out, gs_out,
    img, txt, vt, vs, ert, ect, ers, ecs, wts,
    rmax, rsum, cmax, csum, rel, rst, cst, rall, call, rst_in, cst_in,
    gi_own, gi_snd, gi_in, gt_all, gt_sib, gt_own, gt_snd, gt_in,
    sc_snd, sc_a, sc_mid, sc_b,
    loc_sem, ps_s, ps_r, zs_s, zs_r, cs_s, cs_r,
    rx_s, rx_r, cx_s, cx_r, gi_s, gi_r, sb_s, sb_r, gt_s, gt_r,
    sa_s, sa_r, sb2_s, sb2_r,
):
    g, d = lax.axis_index("grp"), lax.axis_index("dev")
    x, y, z, c = g % 4, d // 4, ((d // 2) % 2) * 4 + g // 4, d % 2
    me_p, me_c = y * 4 + x, z * 2 + c
    sib = 1 - c

    def at(xx, yy, zz, cc):
        return ((zz % 4) * 4 + xx, yy * 4 + (zz // 4) * 2 + cc)

    plane = [(dx, dy) for dy in range(NY) for dx in range(NX) if (dx, dy) != (0, 0)]
    column = [(dz, dc) for dz in range(NZ) for dc in range(2) if (dz, dc) != (0, 0)]

    def plane_peer(dx, dy):
        px, py = (x + dx) % NX, (y + dy) % NY
        return py * 4 + px, at(px, py, z, c)

    def column_peer(dz, dc):
        pz, pc = (z + dz) % NZ, (c + dc) % 2
        return pz * 2 + pc, at(x, y, pz, pc)

    def along(h, axis, step):
        if (h + axis) % 2 == 0:
            return at((x + step) % NX, y, z, c)
        return at(x, (y + step) % NY, z, c)

    def up(step):
        return at(x, y, (z + step) % NZ, c)

    other = at(x, y, z, sib)

    local = []

    def bring(src, dst):
        cp = pltpu.make_async_copy(src, dst, loc_sem.at[len(local)])
        cp.start()
        local.append(cp)

    for h in range(2):
        r = row_unit(h, 0, 0)
        bring(ti.at[pl.ds(32 * h, 32)], img.at[pl.ds(r, 32), pl.ds(0, TW)])
        bring(si.at[pl.ds(32 * h, 32)], img.at[pl.ds(r, 32), pl.ds(TW, SW)])
    bring(tt, txt.at[0, c, :, pl.ds(0, TW)])
    bring(st, txt.at[0, c, :, pl.ds(TW, SW)])

    barrier = pltpu.get_barrier_semaphore()
    near = [along(0, axis, step) for axis in range(2) for step in (1, -1)] + [up(1), up(-1), other]
    for dev in near:
        pl.semaphore_signal(barrier, inc=1, device_id=dev, device_id_type=MESH)
    for cp in local:
        cp.wait()
    pl.semaphore_wait(barrier, len(near))

    sent = []

    def send(src, dst, ssem, rsem, dev):
        cp = pltpu.make_async_remote_copy(
            src_ref=src, dst_ref=dst, send_sem=ssem, recv_sem=rsem, device_id=dev, device_id_type=MESH
        )
        cp.start()
        sent.append(cp)

    def arrived(dst, ssem, rsem, dev):
        pltpu.make_async_remote_copy(
            src_ref=dst, dst_ref=dst, send_sem=ssem, recv_sem=rsem, device_id=dev, device_id_type=MESH
        ).wait_recv()

    both = (1, -1)

    def unit(h, a, b, r0=0, n=32):
        return img.at[pl.ds(row_unit(h, a % 4, b % 4) + r0, n)]

    def sem_id(h, stage, sign, k):
        return 20 * h + (0, 2, 4, 12)[stage] + (sign > 0) + 2 * k

    def psend(h, stage, sign, k, src, dst, axis):
        i = sem_id(h, stage, sign, k)
        send(src, dst, ps_s.at[i], ps_r.at[i], along(h, axis, sign))

    def pwait(h, stage, sign, k, dst, axis):
        i = sem_id(h, stage, sign, k)
        arrived(dst, ps_s.at[i], ps_r.at[i], along(h, axis, -sign))

    def half_of(sign):
        return (0 if sign > 0 else 16), 16

    def s1_send(h):
        for sign in both:
            psend(h, 0, sign, 0, unit(h, 0, 0), unit(h, -sign, 0), 0)

    def s1_recv(h):
        for sign in both:
            pwait(h, 0, sign, 0, unit(h, -sign, 0), 0)
            psend(h, 1, sign, 0, unit(h, -sign, 0, *half_of(sign)), unit(h, 2, 0, *half_of(sign)), 0)
        for sign in both:
            t1_send(h, 1 if sign > 0 else 2)

    def s2_recv(h):
        for sign in both:
            pwait(h, 1, sign, 0, unit(h, 2, 0, *half_of(sign)), 0)
        t1_send(h, 3)

    def t1_send(h, k):
        for sign in both:
            psend(h, 2, sign, k, unit(h, A_OF[k], 0), unit(h, A_OF[k], -sign), 1)

    def t1_recv(h, k):
        for sign in both:
            pwait(h, 2, sign, k, unit(h, A_OF[k], -sign), 1)
            psend(h, 3, sign, k, unit(h, A_OF[k], -sign, *half_of(sign)), unit(h, A_OF[k], 2, *half_of(sign)), 1)

    def t2_recv(h, k):
        for sign in both:
            pwait(h, 3, sign, k, unit(h, A_OF[k], 2, *half_of(sign)), 1)

    def zpart(dz, q):
        return txt.at[SLOT[dz % 8], c, pl.ds(32 * q, 32)]

    def first_half(sign):
        return 0 if sign > 0 else 1

    def z_move(sign, s, q):
        i = ((s - 1) * 2 + q) * 2 + (sign > 0)
        send(zpart(-sign * (s - 1), q), zpart(-sign * s, q), zs_s.at[i], zs_r.at[i], up(sign))

    def z_come(sign, s, q):
        i = ((s - 1) * 2 + q) * 2 + (sign > 0)
        arrived(zpart(-sign * s, q), zs_s.at[i], zs_r.at[i], up(-sign))

    def z_step(s, second):
        for sign in both:
            q = first_half(sign) ^ second
            z_come(sign, s, q)
            if s < 3 or not second:
                z_move(sign, s + 1, q)

    def c_move(dz):
        send(txt.at[SLOT[dz % 8], c], txt.at[SLOT[dz % 8], c], cs_s.at[dz % 8], cs_r.at[dz % 8], other)

    def c_come(dz):
        arrived(txt.at[SLOT[dz % 8], sib], cs_s.at[dz % 8], cs_r.at[dz % 8], other)

    lt, ls = tscale[0] * LOG2E, sscale[0] * LOG2E
    parts = ((0, TW, lt, vt, ert, ect), (TW, W, ls, vs, ers, ecs))

    def tile(q, strip, c0, n):
        r0 = q * CHUNK
        cols = pl.ds(c0, n)
        blocks = pl.ds(c0 // 128, n // 128)
        for part, (lo, hi, scale, raw, er, ec) in enumerate(parts):
            raw[pl.ds(r0, CHUNK), cols] = scale * lax.dot_general(
                img[pl.ds(r0, CHUNK), lo:hi],
                txt[blocks, :, :, lo:hi].reshape(n, hi - lo),
                NT,
                preferred_element_type=jnp.float32,
            )
            peak = None
            for s in range(CHUNK // 32):
                rows = pl.ds(r0 + 32 * s, 32)
                v = raw[rows, cols]
                m = lanes(v, jnp.maximum)
                e = jnp.exp2(v - wide(m, n // 128))
                er[rows, cols] = e
                rmax[part, strip, rows, :] = m
                rsum[part, strip, rows, :] = lanes(e, jnp.add)
                high = sublanes(v, jnp.maximum)
                peak = high if peak is None else jnp.maximum(peak, high)
            total = None
            for s in range(CHUNK // 32):
                rows = pl.ds(r0 + 32 * s, 32)
                e = jnp.exp2(raw[rows, cols] - tall(peak, 4))
                ec[rows, cols] = e
                add = sublanes(e, jnp.add)
                total = add if total is None else total + add
            cmax[part, q, :, cols] = peak
            csum[part, q, :, cols] = total

    def tiles(first, last, strip):
        def body(q, carry):
            tile(q, strip, *STRIPS[strip])
            return carry

        lax.fori_loop(first, last, body, 0)

    for h in range(2):
        s1_send(h)
    for second in range(2):
        for sign in both:
            z_move(sign, 1, first_half(sign) ^ second)
    c_move(0)
    for h in range(2):
        t1_send(h, 0)
    for h in range(2):
        s1_recv(h)
    z_step(1, 0)
    for h in range(2):
        t1_recv(h, 0)
    z_step(1, 1)
    for sign in both:
        c_move(sign)
    for h in range(2):
        s2_recv(h)
    z_step(2, 0)
    for h in range(2):
        t1_recv(h, 1)
    z_step(2, 1)
    for sign in both:
        c_move(2 * sign)
    for h in range(2):
        t1_recv(h, 2)
    for dz in (0, 1, -1, 2):
        c_come(dz)
    tiles(0, 1, 0)
    z_step(3, 0)
    for h in range(2):
        t2_recv(h, 0)
    tiles(1, 2, 0)
    for h in range(2):
        t1_recv(h, 3)
    z_step(3, 1)
    for sign in both:
        c_move(3 * sign)
    tiles(2, 3, 0)
    for dz in (-2, 3):
        c_come(dz)
    tiles(0, 3, 1)
    for sign in both:
        z_come(sign, 4, first_half(sign))
    c_move(4)
    for h in range(2):
        for k in (1, 2, 3):
            t2_recv(h, k)
    for dz in (-3, 4):
        c_come(dz)
    tiles(0, 3, 2)
    for strip, (c0, n) in enumerate(LAST):
        tile(3, strip, c0, n)

    for part in range(2):
        high = jnp.max(cmax[part], axis=0)
        high = jnp.max(high, axis=0, keepdims=True)
        total = jnp.sum(csum[part] * jnp.exp2(cmax[part] - high[None]), axis=0)
        lse = high + jnp.log2(jnp.sum(total, axis=0, keepdims=True))
        for dz in range(8):
            k = SLOT[dz]
            cst[pl.ds(part * 8 + (z + dz) % 8, 1), :] = lse[:, 128 * k:128 * k + 128]
    for dz, dc in column:
        i, dev = column_peer(dz, dc)
        send(cst, cst_in.at[me_c], cx_s.at[i], cx_r.at[me_c], dev)

    for part in range(2):
        for k in range(8):
            rows = pl.ds(128 * k, 128)
            strips = range(3 if k < 6 else 2)
            m = [rmax[part, s, rows, :] for s in strips]
            high = functools.reduce(jnp.maximum, m)
            total = functools.reduce(jnp.add, [rsum[part, s, rows, :] * jnp.exp2(m[s] - high) for s in strips])
            high, total = high.T, total.T
            peak = jnp.max(high, axis=0, keepdims=True)
            lse = peak + jnp.log2(jnp.sum(total * jnp.exp2(high - peak), axis=0, keepdims=True))
            for h, a, b, r in UNITS:
                if r // 128 == k:
                    o = r % 128
                    rel[pl.ds(part * 8 + h * 4 + b, 1), pl.ds(32 * a, 32)] = lse[:, o:o + 32]
        v = rel[pl.ds(part * 8, 8), :]
        v = (pltpu.roll(v, 32 * x, axis=1), pltpu.roll(v, 32 * y, axis=1))
        for h in range(2):
            for b in range(4):
                k = h * 4 + b
                rst[pl.ds(part * 8 + h * 4 + (b + (y, x)[h]) % 4, 1), :] = v[h][k:k + 1]
    for dx, dy in plane:
        i, dev = plane_peer(dx, dy)
        send(rst, rst_in.at[me_p], rx_s.at[i], rx_r.at[me_p], dev)
    cst_in[me_c] = cst[...]
    rst_in[me_p] = rst[...]

    def total_lse(v):
        m = jnp.max(v, axis=0)
        return m + jnp.log2(jnp.sum(jnp.exp2(v - m[None]), axis=0))

    half = 0.5 * sscale[0]
    for dz, dc in column:
        i, dev = column_peer(dz, dc)
        arrived(cst_in.at[i], cx_s.at[i], cx_r.at[i], dev)
    col = total_lse(cst_in[...])
    call[...] = col
    for part in range(2):
        lse = [None] * 8
        for dz in range(8):
            lse[SLOT[dz]] = call[pl.ds(part * 8 + (z + dz) % 8, 1), :]
        cmax[part] = half * jnp.exp2(cmax[part] - jnp.concatenate(lse, axis=1)[None])
    for dx, dy in plane:
        i, dev = plane_peer(dx, dy)
        arrived(rst_in.at[i], rx_s.at[i], rx_r.at[i], dev)
    row = total_lse(rst_in[...])
    rall[...] = row
    for part in range(2):
        for h in range(2):
            for b in range(4):
                rel[pl.ds(part * 8 + h * 4 + b, 1), :] = rall[pl.ds(part * 8 + h * 4 + (b + (y, x)[h]) % 4, 1), :]
        v = rel[pl.ds(part * 8, 8), :]
        v = (pltpu.roll(v, 128 - 32 * x, axis=1), pltpu.roll(v, 128 - 32 * y, axis=1))
        for k in range(8):
            mine = sorted((r, h, a, b) for h, a, b, r in UNITS if r // 128 == k)
            lse = jnp.concatenate(
                [v[h][h * 4 + b:h * 4 + b + 1, 32 * a:32 * a + 32] for _, h, a, b in mine], axis=1
            )
            lse = jnp.broadcast_to(lse, (128, 128)).T
            rows = pl.ds(128 * k, 128)
            for s in range(3 if k < 6 else 2):
                rmax[part, s, rows, :] = half * jnp.exp2(rmax[part, s, rows, :] - lse)

    def pass2(strips):
        def body(s, carry):
            loss_acc, scale_acc = carry
            rows = pl.ds(pl.multiple_of(s * 32, 32), 32)
            q = s // (CHUNK // 32)
            for strip, (c0, n) in enumerate(strips):
                cols = pl.ds(c0, n)
                v = vs[rows, cols]
                k = n // 128
                teach = ert[rows, cols] * wide(rmax[0, strip, rows, :], k) + ect[rows, cols] * tall(cmax[0, q, :, cols], 4)
                stud = ers[rows, cols] * wide(rmax[1, strip, rows, :], k) + ecs[rows, cols] * tall(cmax[1, q, :, cols], 4)
                differ = stud - teach
                wts[rows, cols] = differ.astype(jnp.bfloat16)
                loss_acc = loss_acc + lanes(sublanes(teach * v, jnp.add), jnp.add)
                scale_acc = scale_acc + lanes(sublanes(differ * v, jnp.add), jnp.add)
            return loss_acc, scale_acc

        return body

    zero = jnp.zeros((8, 128), jnp.float32)
    accs = lax.fori_loop(0, 24, pass2(STRIPS), (zero, zero), unroll=2)
    loss_acc, scale_acc = lax.fori_loop(24, 32, pass2(LAST), accs, unroll=2)

    back = LN2 / half
    sc_snd[pl.ds(0, 8), :] = (row[8:, :] + col[8:, :]) * (LN2 / 16.0) - loss_acc * back
    sc_snd[pl.ds(8, 8), :] = scale_acc * back
    for dx, dy in plane:
        i, dev = plane_peer(dx, dy)
        send(sc_snd, sc_a.at[me_p], sa_s.at[i], sa_r.at[me_p], dev)

    for q in (3, 2, 1, 0):
        v = lax.dot_general(
            wts[:, 256 * q:256 * q + 256], img[:, TW:], TN, preferred_element_type=jnp.float32
        )
        pair = pl.ds(2 * q, 2)
        gt_all[pair] = v.reshape(2, 2, ROWS, SW)
        send(gt_all.at[pair, sib], gt_sib.at[pair], sb_s.at[q], sb_r.at[q], other)

    for q in range(4):
        v = jnp.dot(
            wts[pl.ds(256 * q, 256), :], txt[:, :, :, TW:].reshape(TILE, SW), preferred_element_type=jnp.float32
        )
        for h, a, b, r in UNITS:
            if r // 256 == q:
                o = r % 256
                place = (b * 4 + a) if h == 0 else (a * 4 + b)
                gi_snd[place, pl.ds(32 * h, 32), :] = v[o:o + 32].astype(jnp.bfloat16)
                if place == 0:
                    gi_own[pl.ds(32 * h, 32), :] = v[o:o + 32]
    for dx, dy in plane:
        i, dev = plane_peer(dx, dy)
        send(gi_snd.at[dy * 4 + dx], gi_in.at[me_p], gi_s.at[i], gi_r.at[me_p], dev)

    for q in (3, 2, 1, 0):
        pair = pl.ds(2 * q, 2)
        arrived(gt_sib.at[pair], sb_s.at[q], sb_r.at[q], other)
        for dz in range(8):
            k = SLOT[dz]
            if k // 2 == q:
                v = gt_all[k, c] + gt_sib[k]
                if dz == 0:
                    gt_own[...] = v
                else:
                    gt_snd[k] = v.astype(jnp.bfloat16)
                    pz = (z + dz) % 8
                    send(gt_snd.at[k], gt_in.at[z], gt_s.at[pz], gt_r.at[z], at(x, y, pz, c))

    v = sc_snd[...]
    for dx, dy in plane:
        i, dev = plane_peer(dx, dy)
        arrived(sc_a.at[i], sa_s.at[i], sa_r.at[i], dev)
    sc_a[me_p] = v
    sc_mid[...] = jnp.sum(sc_a[...], axis=0)
    for dz, dc in column:
        i, dev = column_peer(dz, dc)
        send(sc_mid, sc_b.at[me_c], sb2_s.at[i], sb2_r.at[me_c], dev)

    gi_out[...] = gi_own[...]
    for dx, dy in plane:
        i, dev = plane_peer(dx, dy)
        arrived(gi_in.at[i], gi_s.at[i], gi_r.at[i], dev)
        gi_out[...] += gi_in[i].astype(jnp.float32)
    gt_out[...] = gt_own[...]
    for dz in range(1, 8):
        pz = (z + dz) % 8
        arrived(gt_in.at[pz], gt_s.at[pz], gt_r.at[pz], at(x, y, pz, c))
        gt_out[...] += gt_in[pz].astype(jnp.float32)
    for dz, dc in column:
        i, dev = column_peer(dz, dc)
        arrived(sc_b.at[i], sb2_s.at[i], sb2_r.at[i], dev)
    sc_b[me_c] = sc_mid[...]
    total = jnp.sum(sc_b[...], axis=0)
    pairs = 2.0 * TILE * 16
    loss_out[0] = jnp.sum(total[:8]) / pairs
    gs_out[0] = jnp.sum(total[8:]) / (pairs * sscale[0])
    for cp in sent:
        cp.wait_send()


def shards(*args):
    f32, bf16 = jnp.float32, jnp.bfloat16
    anyw = pl.BlockSpec(memory_space=pl.ANY)
    vmem = pl.BlockSpec(memory_space=pltpu.VMEM)
    smem = pl.BlockSpec(memory_space=pltpu.SMEM)
    sem = pltpu.SemaphoreType.DMA
    V = pltpu.VMEM
    return tuple(pl.pallas_call(
        kernel,
        out_shape=(
            jax.ShapeDtypeStruct((ROWS, SW), f32),
            jax.ShapeDtypeStruct((ROWS, SW), f32),
            jax.ShapeDtypeStruct((1,), f32),
            jax.ShapeDtypeStruct((1,), f32),
        ),
        in_specs=[anyw] * 4 + [smem] * 2,
        out_specs=(vmem, vmem, smem, smem),
        scratch_shapes=[
            V((TILE, W), bf16),
            V((NZ, 2, ROWS, W), bf16),
            V((TILE, TILE), f32),
            V((TILE, TILE), f32),
            V((TILE, TILE), f32),
            V((TILE, TILE), f32),
            V((TILE, TILE), f32),
            V((TILE, TILE), f32),
            V((TILE, TILE), bf16),
            V((2, 3, TILE, 128), f32),
            V((2, 3, TILE, 128), f32),
            V((2, 4, 8, TILE), f32),
            V((2, 4, 8, TILE), f32),
            V((16, 128), f32),
            V((16, 128), f32),
            V((16, 128), f32),
            V((16, 128), f32),
            V((16, 128), f32),
            V((16, 16, 128), f32),
            V((16, 16, 128), f32),
            V((ROWS, SW), f32),
            V((16, ROWS, SW), bf16),
            V((16, ROWS, SW), bf16),
            V((8, 2, ROWS, SW), f32),
            V((8, ROWS, SW), f32),
            V((ROWS, SW), f32),
            V((8, ROWS, SW), bf16),
            V((8, ROWS, SW), bf16),
            V((16, 128), f32),
            V((16, 16, 128), f32),
            V((16, 128), f32),
            V((16, 16, 128), f32),
            sem((6,)),
            sem((40,)), sem((40,)),
            sem((16,)), sem((16,)),
            sem((8,)), sem((8,)),
            sem((16,)), sem((16,)),
            sem((16,)), sem((16,)),
            sem((16,)), sem((16,)),
            sem((4,)), sem((4,)),
            sem((8,)), sem((8,)),
            sem((16,)), sem((16,)),
            sem((16,)), sem((16,)),
        ],
        compiler_params=pltpu.CompilerParams(
            collective_id=0, has_side_effects=True, vmem_limit_bytes=60 * 1024 * 1024
        ),
    )(*args))


def solution(mesh):
    return jax.shard_map(
        shards,
        mesh=mesh,
        in_specs=(
            P(("grp", "dev"), None),
            P(("grp", "dev"), None),
            P(("grp", "dev"), None),
            P(("grp", "dev"), None),
            P(),
            P(),
        ),
        out_specs=(P(("grp", "dev"), None), P(("grp", "dev"), None), P(), P()),
        check_vma=False,
    )
```

```python
import functools

import jax
import jax.numpy as jnp
from jax import lax
from jax.experimental import pallas as pl
from jax.experimental.pallas import tpu as pltpu
from jax.sharding import PartitionSpec as P

NX, NY, NZ = 4, 4, 8
ROWS = 64
TW, SW = 1280, 512
W = TW + SW
TILE = 1024
CHUNK = 256
LOG2E = 1.4426950408889634
LN2 = 0.6931471805599453
MESH = pl.DeviceIdType.MESH
NT = (((1,), (1,)), ((), ()))
TN = (((0,), (0,)), ((), ()))

A_OF = (0, 3, 1, 2)
SLOT = (0, 1, 3, 5, 7, 6, 4, 2)
STRIPS = ((0, 512), (512, 256), (768, 256))
LAST = ((0, 512), (512, 512))


def row_unit(h, a, b):
    k = A_OF.index(a)
    if b == 0:
        return 128 * h + 32 * a
    if b == 2:
        return 768 + 64 * k + 32 * h
    return 256 + 128 * k + (0 if b == 3 else 64) + 32 * h


UNITS = tuple((h, a, b, row_unit(h, a, b)) for h in range(2) for a in range(4) for b in range(4))


def lanes(v, op):
    return functools.reduce(op, [v[:, 128 * k:128 * k + 128] for k in range(v.shape[1] // 128)])


def sublanes(v, op):
    return functools.reduce(op, [v[8 * k:8 * k + 8] for k in range(v.shape[0] // 8)])


def wide(v, n):
    return jnp.concatenate([v] * n, axis=1)


def tall(v, n):
    return jnp.concatenate([v] * n, axis=0)


def kernel(
    ti, tt, si, st, tscale, sscale,
    gi_out, gt_out, loss_out, gs_out,
    img, txt, vt, vs, ert, ect, ers, ecs, wts,
    rmax, rsum, cmax, csum, rel, rst, cst, rall, call, rst_in, cst_in,
    gi_own, gi_mid, gi_snd, gi_in, g2_snd, g2_in, gt_all, gt_sib, gt_snd, gt_in,
    sc_snd, sc_in,
    loc_sem, ps_s, ps_r, zs_s, zs_r, cs_s, cs_r,
    rx_s, rx_r, cx_s, cx_r, g1_s, g1_r, g2_s, g2_r, sb_s, sb_r, gt_s, gt_r,
    sc_s, sc_r,
):
    g, d = lax.axis_index("grp"), lax.axis_index("dev")
    x, y, z, c = g % 4, d // 4, ((d // 2) % 2) * 4 + g // 4, d % 2
    me_p, me_c = y * 4 + x, z * 2 + c
    sib = 1 - c

    def at(xx, yy, zz, cc):
        return ((zz % 4) * 4 + xx, yy * 4 + (zz // 4) * 2 + cc)

    plane = [(dx, dy) for dy in range(NY) for dx in range(NX) if (dx, dy) != (0, 0)]
    column = [(dz, dc) for dz in range(NZ) for dc in range(2) if (dz, dc) != (0, 0)]

    def plane_peer(dx, dy):
        px, py = (x + dx) % NX, (y + dy) % NY
        return py * 4 + px, at(px, py, z, c)

    def column_peer(dz, dc):
        pz, pc = (z + dz) % NZ, (c + dc) % 2
        return pz * 2 + pc, at(x, y, pz, pc)

    def along(h, axis, step):
        if (h + axis) % 2 == 0:
            return at((x + step) % NX, y, z, c)
        return at(x, (y + step) % NY, z, c)

    def up(step):
        return at(x, y, (z + step) % NZ, c)

    other = at(x, y, z, sib)

    local = []

    def bring(src, dst):
        cp = pltpu.make_async_copy(src, dst, loc_sem.at[len(local)])
        cp.start()
        local.append(cp)

    for h in range(2):
        r = row_unit(h, 0, 0)
        bring(ti.at[pl.ds(32 * h, 32)], img.at[pl.ds(r, 32), pl.ds(0, TW)])
        bring(si.at[pl.ds(32 * h, 32)], img.at[pl.ds(r, 32), pl.ds(TW, SW)])
    bring(tt, txt.at[0, c, :, pl.ds(0, TW)])
    bring(st, txt.at[0, c, :, pl.ds(TW, SW)])

    barrier = pltpu.get_barrier_semaphore()
    near = [along(0, axis, step) for axis in range(2) for step in (1, -1)] + [up(1), up(-1), other]
    for dev in near:
        pl.semaphore_signal(barrier, inc=1, device_id=dev, device_id_type=MESH)
    for cp in local:
        cp.wait()
    pl.semaphore_wait(barrier, len(near))

    sent = []

    def send(src, dst, ssem, rsem, dev):
        cp = pltpu.make_async_remote_copy(
            src_ref=src, dst_ref=dst, send_sem=ssem, recv_sem=rsem, device_id=dev, device_id_type=MESH
        )
        cp.start()
        sent.append(cp)

    def arrived(dst, ssem, rsem, dev):
        pltpu.make_async_remote_copy(
            src_ref=dst, dst_ref=dst, send_sem=ssem, recv_sem=rsem, device_id=dev, device_id_type=MESH
        ).wait_recv()

    both = (1, -1)

    def unit(h, a, b, r0=0, n=32):
        return img.at[pl.ds(row_unit(h, a % 4, b % 4) + r0, n)]

    def sem_id(h, stage, sign, k):
        return 20 * h + (0, 2, 4, 12)[stage] + (sign > 0) + 2 * k

    def psend(h, stage, sign, k, src, dst, axis):
        i = sem_id(h, stage, sign, k)
        send(src, dst, ps_s.at[i], ps_r.at[i], along(h, axis, sign))

    def pwait(h, stage, sign, k, dst, axis):
        i = sem_id(h, stage, sign, k)
        arrived(dst, ps_s.at[i], ps_r.at[i], along(h, axis, -sign))

    def half_of(sign):
        return (0 if sign > 0 else 16), 16

    def s1_send(h):
        for sign in both:
            psend(h, 0, sign, 0, unit(h, 0, 0), unit(h, -sign, 0), 0)

    def s1_recv(h):
        for sign in both:
            pwait(h, 0, sign, 0, unit(h, -sign, 0), 0)
            psend(h, 1, sign, 0, unit(h, -sign, 0, *half_of(sign)), unit(h, 2, 0, *half_of(sign)), 0)
        for sign in both:
            t1_send(h, 1 if sign > 0 else 2)

    def s2_recv(h):
        for sign in both:
            pwait(h, 1, sign, 0, unit(h, 2, 0, *half_of(sign)), 0)
        t1_send(h, 3)

    def t1_send(h, k):
        for sign in both:
            psend(h, 2, sign, k, unit(h, A_OF[k], 0), unit(h, A_OF[k], -sign), 1)

    def t1_recv(h, k):
        for sign in both:
            pwait(h, 2, sign, k, unit(h, A_OF[k], -sign), 1)
            psend(h, 3, sign, k, unit(h, A_OF[k], -sign, *half_of(sign)), unit(h, A_OF[k], 2, *half_of(sign)), 1)

    def t2_recv(h, k):
        for sign in both:
            pwait(h, 3, sign, k, unit(h, A_OF[k], 2, *half_of(sign)), 1)

    def zpart(dz, q):
        return txt.at[SLOT[dz % 8], c, pl.ds(32 * q, 32)]

    def first_half(sign):
        return 0 if sign > 0 else 1

    def z_move(sign, s, q):
        i = ((s - 1) * 2 + q) * 2 + (sign > 0)
        send(zpart(-sign * (s - 1), q), zpart(-sign * s, q), zs_s.at[i], zs_r.at[i], up(sign))

    def z_come(sign, s, q):
        i = ((s - 1) * 2 + q) * 2 + (sign > 0)
        arrived(zpart(-sign * s, q), zs_s.at[i], zs_r.at[i], up(-sign))

    def z_step(s, second):
        for sign in both:
            q = first_half(sign) ^ second
            z_come(sign, s, q)
            if s < 3 or not second:
                z_move(sign, s + 1, q)

    def c_move(dz):
        send(txt.at[SLOT[dz % 8], c], txt.at[SLOT[dz % 8], c], cs_s.at[dz % 8], cs_r.at[dz % 8], other)

    def c_come(dz):
        arrived(txt.at[SLOT[dz % 8], sib], cs_s.at[dz % 8], cs_r.at[dz % 8], other)

    lt, ls = tscale[0] * LOG2E, sscale[0] * LOG2E
    parts = ((0, TW, lt, vt, ert, ect), (TW, W, ls, vs, ers, ecs))

    def tile(q, strip, c0, n):
        r0 = q * CHUNK
        cols = pl.ds(c0, n)
        blocks = pl.ds(c0 // 128, n // 128)
        for part, (lo, hi, scale, raw, er, ec) in enumerate(parts):
            raw[pl.ds(r0, CHUNK), cols] = scale * lax.dot_general(
                img[pl.ds(r0, CHUNK), lo:hi],
                txt[blocks, :, :, lo:hi].reshape(n, hi - lo),
                NT,
                preferred_element_type=jnp.float32,
            )
            peak = None
            for s in range(CHUNK // 32):
                rows = pl.ds(r0 + 32 * s, 32)
                v = raw[rows, cols]
                m = lanes(v, jnp.maximum)
                e = jnp.exp2(v - wide(m, n // 128))
                er[rows, cols] = e
                rmax[part, strip, rows, :] = m
                rsum[part, strip, rows, :] = lanes(e, jnp.add)
                high = sublanes(v, jnp.maximum)
                peak = high if peak is None else jnp.maximum(peak, high)
            total = None
            for s in range(CHUNK // 32):
                rows = pl.ds(r0 + 32 * s, 32)
                e = jnp.exp2(raw[rows, cols] - tall(peak, 4))
                ec[rows, cols] = e
                add = sublanes(e, jnp.add)
                total = add if total is None else total + add
            cmax[part, q, :, cols] = peak
            csum[part, q, :, cols] = total

    def tiles(first, last, strip):
        def body(q, carry):
            tile(q, strip, *STRIPS[strip])
            return carry

        lax.fori_loop(first, last, body, 0)

    for h in range(2):
        s1_send(h)
    for second in range(2):
        for sign in both:
            z_move(sign, 1, first_half(sign) ^ second)
    c_move(0)
    for h in range(2):
        t1_send(h, 0)
    for h in range(2):
        s1_recv(h)
    z_step(1, 0)
    for h in range(2):
        t1_recv(h, 0)
    z_step(1, 1)
    for sign in both:
        c_move(sign)
    for h in range(2):
        s2_recv(h)
    z_step(2, 0)
    for h in range(2):
        t1_recv(h, 1)
    z_step(2, 1)
    for sign in both:
        c_move(2 * sign)
    for h in range(2):
        t1_recv(h, 2)
    for dz in (0, 1, -1, 2):
        c_come(dz)
    tiles(0, 1, 0)
    z_step(3, 0)
    for h in range(2):
        t2_recv(h, 0)
    tiles(1, 2, 0)
    for h in range(2):
        t1_recv(h, 3)
    z_step(3, 1)
    for sign in both:
        c_move(3 * sign)
    tiles(2, 3, 0)
    for dz in (-2, 3):
        c_come(dz)
    tiles(0, 3, 1)
    for sign in both:
        z_come(sign, 4, first_half(sign))
    c_move(4)
    for h in range(2):
        for k in (1, 2, 3):
            t2_recv(h, k)
    tile(3, 0, *LAST[0])
    for dz in (-3, 4):
        c_come(dz)
    tiles(0, 3, 2)
    tile(3, 1, *LAST[1])

    for part in range(2):
        high = jnp.max(cmax[part], axis=0)
        high = jnp.max(high, axis=0, keepdims=True)
        total = jnp.sum(csum[part] * jnp.exp2(cmax[part] - high[None]), axis=0)
        lse = high + jnp.log2(jnp.sum(total, axis=0, keepdims=True))
        for dz in range(8):
            k = SLOT[dz]
            cst[pl.ds(part * 8 + (z + dz) % 8, 1), :] = lse[:, 128 * k:128 * k + 128]
    for dz, dc in column:
        i, dev = column_peer(dz, dc)
        send(cst, cst_in.at[me_c], cx_s.at[i], cx_r.at[me_c], dev)

    for part in range(2):
        for k in range(8):
            rows = pl.ds(128 * k, 128)
            strips = range(3 if k < 6 else 2)
            m = [rmax[part, s, rows, :] for s in strips]
            high = functools.reduce(jnp.maximum, m)
            total = functools.reduce(jnp.add, [rsum[part, s, rows, :] * jnp.exp2(m[s] - high) for s in strips])
            high, total = high.T, total.T
            peak = jnp.max(high, axis=0, keepdims=True)
            lse = peak + jnp.log2(jnp.sum(total * jnp.exp2(high - peak), axis=0, keepdims=True))
            for h, a, b, r in UNITS:
                if r // 128 == k:
                    o = r % 128
                    rel[pl.ds(part * 8 + h * 4 + b, 1), pl.ds(32 * a, 32)] = lse[:, o:o + 32]
        v = rel[pl.ds(part * 8, 8), :]
        v = (pltpu.roll(v, 32 * x, axis=1), pltpu.roll(v, 32 * y, axis=1))
        for h in range(2):
            for b in range(4):
                k = h * 4 + b
                rst[pl.ds(part * 8 + h * 4 + (b + (y, x)[h]) % 4, 1), :] = v[h][k:k + 1]
    for dx, dy in plane:
        i, dev = plane_peer(dx, dy)
        send(rst, rst_in.at[me_p], rx_s.at[i], rx_r.at[me_p], dev)
    cst_in[me_c] = cst[...]
    rst_in[me_p] = rst[...]

    def total_lse(v):
        m = jnp.max(v, axis=0)
        return m + jnp.log2(jnp.sum(jnp.exp2(v - m[None]), axis=0))

    half = 0.5 * sscale[0]
    for dz, dc in column:
        i, dev = column_peer(dz, dc)
        arrived(cst_in.at[i], cx_s.at[i], cx_r.at[i], dev)
    col = total_lse(cst_in[...])
    call[...] = col
    for part in range(2):
        lse = [None] * 8
        for dz in range(8):
            lse[SLOT[dz]] = call[pl.ds(part * 8 + (z + dz) % 8, 1), :]
        cmax[part] = half * jnp.exp2(cmax[part] - jnp.concatenate(lse, axis=1)[None])
    for dx, dy in plane:
        i, dev = plane_peer(dx, dy)
        arrived(rst_in.at[i], rx_s.at[i], rx_r.at[i], dev)
    row = total_lse(rst_in[...])
    rall[...] = row
    for part in range(2):
        for h in range(2):
            for b in range(4):
                rel[pl.ds(part * 8 + h * 4 + b, 1), :] = rall[pl.ds(part * 8 + h * 4 + (b + (y, x)[h]) % 4, 1), :]
        v = rel[pl.ds(part * 8, 8), :]
        v = (pltpu.roll(v, 128 - 32 * x, axis=1), pltpu.roll(v, 128 - 32 * y, axis=1))
        for k in range(8):
            mine = sorted((r, h, a, b) for h, a, b, r in UNITS if r // 128 == k)
            lse = jnp.concatenate(
                [v[h][h * 4 + b:h * 4 + b + 1, 32 * a:32 * a + 32] for _, h, a, b in mine], axis=1
            )
            lse = jnp.broadcast_to(lse, (128, 128)).T
            rows = pl.ds(128 * k, 128)
            for s in range(3 if k < 6 else 2):
                rmax[part, s, rows, :] = half * jnp.exp2(rmax[part, s, rows, :] - lse)

    def pass2(c0, n, head, last, carry):
        cols = pl.ds(c0, n)
        k = n // 128

        def body(s, carry, strip):
            loss_acc, scale_acc = carry
            rows = pl.ds(pl.multiple_of(s * 32, 32), 32)
            q = s // (CHUNK // 32)
            v = vs[rows, cols]
            teach = ert[rows, cols] * wide(rmax[0, strip, rows, :], k) + ect[rows, cols] * tall(cmax[0, q, :, cols], 4)
            stud = ers[rows, cols] * wide(rmax[1, strip, rows, :], k) + ecs[rows, cols] * tall(cmax[1, q, :, cols], 4)
            differ = stud - teach
            wts[rows, cols] = differ.astype(jnp.bfloat16)
            loss_acc = loss_acc + lanes(sublanes(teach * v, jnp.add), jnp.add)
            scale_acc = scale_acc + lanes(sublanes(differ * v, jnp.add), jnp.add)
            return loss_acc, scale_acc

        carry = lax.fori_loop(0, 24, functools.partial(body, strip=head), carry, unroll=4)
        return lax.fori_loop(24, 32, functools.partial(body, strip=last), carry, unroll=4)

    def text_parts(q):
        v = lax.dot_general(
            wts[:, 256 * q:256 * q + 256], img[:, TW:], TN, preferred_element_type=jnp.float32
        )
        pair = pl.ds(2 * q, 2)
        gt_all[pair] = v.reshape(2, 2, ROWS, SW)
        send(gt_all.at[pair, sib], gt_sib.at[pair], sb_s.at[q], sb_r.at[q], other)

    def text_both(q):
        arrived(gt_sib.at[pl.ds(2 * q, 2)], sb_s.at[q], sb_r.at[q], other)

    def own_part(dz, q):
        rows = pl.ds(32 * q, 32)
        return gt_all[SLOT[dz % 8], c, rows, :] + gt_sib[SLOT[dz % 8], rows, :]

    def chain_ref(ref, sign, s, q):
        return ref.at[s * 2 + (sign > 0), pl.ds(32 * q, 32)]

    def chain_id(sign, s, q):
        return (s * 2 + q) * 2 + (sign > 0)

    def chain_wait(sign, s, q):
        i = chain_id(sign, s, q)
        arrived(chain_ref(gt_in, sign, s, q), gt_s.at[i], gt_r.at[i], up(-sign))
        return chain_ref(gt_in, sign, s, q)[...].astype(jnp.float32)

    def chain_send(sign, s, q):
        v = own_part(sign * (3 - s), q)
        if s > 0:
            v = v + chain_wait(sign, s - 1, q)
        chain_ref(gt_snd, sign, s, q)[...] = v.astype(jnp.bfloat16)
        i = chain_id(sign, s, q)
        send(chain_ref(gt_snd, sign, s, q), chain_ref(gt_in, sign, s, q), gt_s.at[i], gt_r.at[i], up(sign))

    def far_send():
        for q in range(2):
            gt_snd[6, pl.ds(32 * q, 32)] = own_part(4, q).astype(jnp.bfloat16)
        send(gt_snd.at[6], gt_in.at[6], gt_s.at[12], gt_r.at[12], up(4))

    def far_wait():
        arrived(gt_in.at[6], gt_s.at[12], gt_r.at[12], up(4))
        return gt_in[6].astype(jnp.float32)

    def image_parts(q):
        v = jnp.dot(
            wts[pl.ds(256 * q, 256), :], txt[:, :, :, TW:].reshape(TILE, SW), preferred_element_type=jnp.float32
        )
        for h, a, b, r in UNITS:
            if r // 256 == q:
                o = r % 256
                if b == 0:
                    gi_own[h, a] = v[o:o + 32]
                else:
                    gi_snd[h, b, a] = v[o:o + 32].astype(jnp.bfloat16)

    pieces = ((2, 2), (1, 1), (0, 1))

    def stage1_id(h, b, p):
        return (h * 4 + b) * 3 + p

    def stage1_send(b, p):
        for h in range(2):
            i = stage1_id(h, 4 - b, p)
            part = pl.ds(*pieces[p])
            send(gi_snd.at[h, b, part], gi_in.at[h, 4 - b, part], g1_s.at[i], g1_r.at[i], along(h, 1, b))

    def stage1_sum(h, p):
        first_a, count = pieces[p]
        for b in range(1, 4):
            i = stage1_id(h, b, p)
            arrived(gi_in.at[h, b, pl.ds(first_a, count)], g1_s.at[i], g1_r.at[i], along(h, 1, b))
        for a in range(first_a, first_a + count):
            v = gi_own[h, a] + gi_in[h, 1, a].astype(jnp.float32)
            v = v + gi_in[h, 2, a].astype(jnp.float32) + gi_in[h, 3, a].astype(jnp.float32)
            if a == 0:
                gi_mid[h] = v
            else:
                g2_snd[h, a] = v.astype(jnp.bfloat16)
                i = h * 4 + 4 - a
                send(g2_snd.at[h, a], g2_in.at[h, 4 - a], g2_s.at[i], g2_r.at[i], along(h, 0, a))

    def stage2_sum(h):
        v = gi_mid[h]
        for a in range(1, 4):
            i = h * 4 + a
            arrived(g2_in.at[h, a], g2_s.at[i], g2_r.at[i], along(h, 0, a))
            v = v + g2_in[h, a].astype(jnp.float32)
        gi_out[pl.ds(32 * h, 32), :] = v

    def scalar_send(level, peers, peer, me):
        for p in peers:
            i, dev = peer(*p)
            send(sc_snd.at[level], sc_in.at[level, me], sc_s.at[level, i], sc_r.at[level, me], dev)

    def scalar_sum(level, peers, peer, me):
        v = sc_snd[level]
        for p in peers:
            i, dev = peer(*p)
            arrived(sc_in.at[level, i], sc_s.at[level, i], sc_r.at[level, i], dev)
            v = v + sc_in[level, i]
        return v

    in_plane = (plane, plane_peer, me_p)
    in_column = (column, column_peer, me_c)

    zero = jnp.zeros((8, 128), jnp.float32)
    accs = pass2(768, 256, 2, 1, (zero, zero))
    text_parts(3)
    accs = pass2(512, 256, 1, 1, accs)
    text_parts(2)
    loss_acc, scale_acc = pass2(0, 512, 0, 0, accs)

    back = LN2 / half
    loss_acc = (row[8:, :] + col[8:, :]) * (LN2 / 16.0) - loss_acc * back
    sc_snd[0, pl.ds(0, 1), :] = jnp.sum(loss_acc, axis=0, keepdims=True)
    sc_snd[0, pl.ds(1, 1), :] = jnp.sum(scale_acc * back, axis=0, keepdims=True)
    scalar_send(0, *in_plane)

    text_both(3)
    for q in range(2):
        chain_send(-1, 0, q)
    image_parts(3)
    for p in range(3):
        stage1_send(2, p)
    image_parts(1)
    image_parts(2)
    for p in range(3):
        for b in (1, 3):
            stage1_send(b, p)
    text_both(2)
    for q in range(2):
        chain_send(1, 0, q)

    text_parts(1)
    text_parts(0)
    image_parts(0)
    sc_snd[1] = scalar_sum(0, *in_plane)
    scalar_send(1, *in_column)
    far_send()
    text_both(1)
    for q in range(2):
        for sign in (-1, 1):
            chain_send(sign, 1, q)
    for h in range(2):
        stage1_sum(h, 0)
    text_both(0)
    for q in range(2):
        for sign in (-1, 1):
            chain_send(sign, 2, q)
    for h in range(2):
        stage1_sum(h, 1)
    far = far_wait()
    for h in range(2):
        stage1_sum(h, 2)
    total = scalar_sum(1, *in_column)
    for q in range(2):
        v = own_part(0, q) + far[32 * q:32 * q + 32]
        for sign in both:
            v = v + chain_wait(sign, 2, q)
        gt_out[pl.ds(32 * q, 32), :] = v
    for h in range(2):
        stage2_sum(h)
    pairs = 2.0 * TILE * 16
    loss_out[0] = jnp.sum(total[:1]) / pairs
    gs_out[0] = jnp.sum(total[1:]) / (pairs * sscale[0])
    for cp in sent:
        cp.wait_send()


def shards(*args):
    f32, bf16 = jnp.float32, jnp.bfloat16
    anyw = pl.BlockSpec(memory_space=pl.ANY)
    vmem = pl.BlockSpec(memory_space=pltpu.VMEM)
    smem = pl.BlockSpec(memory_space=pltpu.SMEM)
    sem = pltpu.SemaphoreType.DMA
    V = pltpu.VMEM
    return tuple(pl.pallas_call(
        kernel,
        out_shape=(
            jax.ShapeDtypeStruct((ROWS, SW), f32),
            jax.ShapeDtypeStruct((ROWS, SW), f32),
            jax.ShapeDtypeStruct((1,), f32),
            jax.ShapeDtypeStruct((1,), f32),
        ),
        in_specs=[anyw] * 4 + [smem] * 2,
        out_specs=(vmem, vmem, smem, smem),
        scratch_shapes=[
            V((TILE, W), bf16),
            V((NZ, 2, ROWS, W), bf16),
            V((TILE, TILE), f32),
            V((TILE, TILE), f32),
            V((TILE, TILE), f32),
            V((TILE, TILE), f32),
            V((TILE, TILE), f32),
            V((TILE, TILE), f32),
            V((TILE, TILE), bf16),
            V((2, 3, TILE, 128), f32),
            V((2, 3, TILE, 128), f32),
            V((2, 4, 8, TILE), f32),
            V((2, 4, 8, TILE), f32),
            V((16, 128), f32),
            V((16, 128), f32),
            V((16, 128), f32),
            V((16, 128), f32),
            V((16, 128), f32),
            V((16, 16, 128), f32),
            V((16, 16, 128), f32),
            V((2, 4, 32, SW), f32),
            V((2, 32, SW), f32),
            V((2, 4, 4, 32, SW), bf16),
            V((2, 4, 4, 32, SW), bf16),
            V((2, 4, 32, SW), bf16),
            V((2, 4, 32, SW), bf16),
            V((8, 2, ROWS, SW), f32),
            V((8, ROWS, SW), f32),
            V((8, ROWS, SW), bf16),
            V((8, ROWS, SW), bf16),
            V((2, 2, 128), f32),
            V((2, 16, 2, 128), f32),
            sem((6,)),
            sem((40,)), sem((40,)),
            sem((16,)), sem((16,)),
            sem((8,)), sem((8,)),
            sem((16,)), sem((16,)),
            sem((16,)), sem((16,)),
            sem((24,)), sem((24,)),
            sem((8,)), sem((8,)),
            sem((4,)), sem((4,)),
            sem((16,)), sem((16,)),
            sem((2, 16)), sem((2, 16)),
        ],
        compiler_params=pltpu.CompilerParams(
            collective_id=0, has_side_effects=True, vmem_limit_bytes=60 * 1024 * 1024
        ),
    )(*args))


def solution(mesh):
    return jax.shard_map(
        shards,
        mesh=mesh,
        in_specs=(
            P(("grp", "dev"), None),
            P(("grp", "dev"), None),
            P(("grp", "dev"), None),
            P(("grp", "dev"), None),
            P(),
            P(),
        ),
        out_specs=(P(("grp", "dev"), None), P(("grp", "dev"), None), P(), P()),
        check_vma=False,
    )
```

```python
import functools

import jax
import jax.numpy as jnp
from jax import lax
from jax.experimental import pallas as pl
from jax.experimental.pallas import tpu as pltpu
from jax.sharding import PartitionSpec as P

NX, NY, NZ = 4, 4, 8
ROWS = 64
TW, SW = 1280, 512
W = TW + SW
TILE = 1024
CHUNK = 256
LOG2E = 1.4426950408889634
LN2 = 0.6931471805599453
MESH = pl.DeviceIdType.MESH
NT = (((1,), (1,)), ((), ()))
TN = (((0,), (0,)), ((), ()))

A_OF = (0, 3, 1, 2)
SLOT = (0, 1, 3, 5, 7, 6, 4, 2)
STRIPS = ((0, 512), (512, 256), (768, 256))
LAST = ((0, 512), (512, 512))


def row_unit(h, a, b):
    k = A_OF.index(a)
    if b == 0:
        return 128 * h + 32 * a
    if b == 2:
        return 768 + 64 * k + 32 * h
    return 256 + 128 * k + (0 if b == 3 else 64) + 32 * h


UNITS = tuple((h, a, b, row_unit(h, a, b)) for h in range(2) for a in range(4) for b in range(4))


def lanes(v, op):
    return functools.reduce(op, [v[:, 128 * k:128 * k + 128] for k in range(v.shape[1] // 128)])


def sublanes(v, op):
    return functools.reduce(op, [v[8 * k:8 * k + 8] for k in range(v.shape[0] // 8)])


def wide(v, n):
    return jnp.concatenate([v] * n, axis=1)


def tall(v, n):
    return jnp.concatenate([v] * n, axis=0)


def kernel(
    ti, tt, si, st, tscale, sscale,
    gi_out, gt_out, sums_out,
    img, txt, vt, vs, ert, ect, ers, ecs, wts,
    rmax, rsum, cmax, csum, rel, rst, cst, rall, call, rst_in, cst_in,
    gi_own, gi_mid, gi_snd, gi_in, g2_snd, g2_in, gt_all, gt_sib, gt_snd, gt_in,
    sc_snd, sc_in,
    loc_sem, ps_s, ps_r, zs_s, zs_r, cs_s, cs_r,
    rx_s, rx_r, cx_s, cx_r, g1_s, g1_r, g2_s, g2_r, sb_s, sb_r, gt_s, gt_r,
    sc_s, sc_r,
):
    g, d = lax.axis_index("grp"), lax.axis_index("dev")
    x, y, z, c = g % 4, d // 4, ((d // 2) % 2) * 4 + g // 4, d % 2
    me_p, me_c = y * 4 + x, z * 2 + c
    sib = 1 - c

    def at(xx, yy, zz, cc):
        return ((zz % 4) * 4 + xx, yy * 4 + (zz // 4) * 2 + cc)

    plane = [(dx, dy) for dy in range(NY) for dx in range(NX) if (dx, dy) != (0, 0)]
    column = [(dz, dc) for dz in range(NZ) for dc in range(2) if (dz, dc) != (0, 0)]

    def plane_peer(dx, dy):
        px, py = (x + dx) % NX, (y + dy) % NY
        return py * 4 + px, at(px, py, z, c)

    def column_peer(dz, dc):
        pz, pc = (z + dz) % NZ, (c + dc) % 2
        return pz * 2 + pc, at(x, y, pz, pc)

    def along(h, axis, step):
        if (h + axis) % 2 == 0:
            return at((x + step) % NX, y, z, c)
        return at(x, (y + step) % NY, z, c)

    def up(step):
        return at(x, y, (z + step) % NZ, c)

    other = at(x, y, z, sib)

    local = []

    def bring(src, dst):
        cp = pltpu.make_async_copy(src, dst, loc_sem)
        cp.start()
        local.append(cp)

    for h in range(2):
        r = row_unit(h, 0, 0)
        bring(ti.at[pl.ds(32 * h, 32)], img.at[pl.ds(r, 32), pl.ds(0, TW)])
        bring(si.at[pl.ds(32 * h, 32)], img.at[pl.ds(r, 32), pl.ds(TW, SW)])
    bring(tt, txt.at[0, c, :, pl.ds(0, TW)])
    bring(st, txt.at[0, c, :, pl.ds(TW, SW)])

    barrier = pltpu.get_barrier_semaphore()
    near = [along(0, axis, step) for axis in range(2) for step in (1, -1)] + [up(1), up(-1), other]
    for dev in near:
        pl.semaphore_signal(barrier, inc=1, device_id=dev, device_id_type=MESH)
    pltpu.make_async_copy(img.at[pl.ds(0, 2 * ROWS)], img.at[pl.ds(0, 2 * ROWS)], loc_sem).wait()
    pl.semaphore_wait(barrier, len(near))

    def remote(src, dst, ssem, rsem, dev):
        return pltpu.make_async_remote_copy(
            src_ref=src, dst_ref=dst, send_sem=ssem, recv_sem=rsem, device_id=dev, device_id_type=MESH
        )

    def send(src, dst, ssem, rsem, dev):
        remote(src, dst, ssem, rsem, dev).start()

    def arrived(like, ssem, rsem):
        remote(like, like, ssem, rsem, other).wait_recv()

    def all_sent(like, ssem, rsem):
        remote(like, like, ssem, rsem, other).wait_send()

    both = (1, -1)

    def unit(h, a, b, r0=0, n=32):
        return img.at[pl.ds(row_unit(h, a % 4, b % 4) + r0, n)]

    def psend(h, i, sign, src, dst, axis):
        send(src, dst, ps_s, ps_r.at[i], along(h, axis, sign))

    def pwait(i, n):
        arrived(img.at[pl.ds(0, n)], ps_s, ps_r.at[i])

    def half_of(sign):
        return (0 if sign > 0 else 16), 16

    hs = [(h, sign) for h in range(2) for sign in both]

    def s1_send():
        for h, sign in hs:
            psend(h, 0, sign, unit(h, 0, 0), unit(h, -sign, 0), 0)

    def s1_recv():
        pwait(0, 128)
        for h, sign in hs:
            psend(h, 1, sign, unit(h, -sign, 0, *half_of(sign)), unit(h, 2, 0, *half_of(sign)), 0)
        t1_send(1)
        t1_send(2)

    def s2_recv():
        pwait(1, 64)
        t1_send(3)

    def t1_send(k):
        for h, sign in hs:
            psend(h, 2 + k, sign, unit(h, A_OF[k], 0), unit(h, A_OF[k], -sign), 1)

    def t1_recv(k):
        pwait(2 + k, 128)
        for h, sign in hs:
            psend(h, 6, sign, unit(h, A_OF[k], -sign, *half_of(sign)), unit(h, A_OF[k], 2, *half_of(sign)), 1)

    def t2_recv():
        pwait(6, 256)

    def zpart(dz, q):
        return txt.at[SLOT[dz % 8], c, pl.ds(32 * q, 32)]

    def first_half(sign):
        return 0 if sign > 0 else 1

    def z_move(sign, s, second):
        q = first_half(sign) ^ second
        send(zpart(-sign * (s - 1), q), zpart(-sign * s, q), zs_s, zs_r.at[(s - 1) * 2 + second], up(sign))

    def z_step(s, second):
        arrived(txt.at[0, 0], zs_s, zs_r.at[(s - 1) * 2 + second])
        for sign in both:
            if s < 3 or (s == 3 and not second):
                z_move(sign, s + 1, second)

    groups = ((0, 4), (4, 2), (6, 2))

    def c_move(dz):
        k = SLOT[dz % 8]
        i = (k >= 4) + (k >= 6)
        send(txt.at[k, c], txt.at[k, c], cs_s, cs_r.at[i], other)

    def c_come(i):
        arrived(txt.at[pl.ds(*groups[i]), sib], cs_s, cs_r.at[i])

    lt, ls = tscale[0] * LOG2E, sscale[0] * LOG2E
    parts = ((0, TW, lt, vt, ert, ect), (TW, W, ls, vs, ers, ecs))

    def tile(q, strip, c0, n):
        r0 = q * CHUNK
        cols = pl.ds(c0, n)
        blocks = pl.ds(c0 // 128, n // 128)
        for part, (lo, hi, scale, raw, er, ec) in enumerate(parts):
            raw[pl.ds(r0, CHUNK), cols] = scale * lax.dot_general(
                img[pl.ds(r0, CHUNK), lo:hi],
                txt[blocks, :, :, lo:hi].reshape(n, hi - lo),
                NT,
                preferred_element_type=jnp.float32,
            )
            peak = None
            for s in range(CHUNK // 32):
                rows = pl.ds(r0 + 32 * s, 32)
                v = raw[rows, cols]
                m = lanes(v, jnp.maximum)
                e = jnp.exp2(v - wide(m, n // 128))
                er[rows, cols] = e
                rmax[part, strip, rows, :] = m
                rsum[part, strip, rows, :] = lanes(e, jnp.add)
                high = sublanes(v, jnp.maximum)
                peak = high if peak is None else jnp.maximum(peak, high)
            total = None
            for s in range(CHUNK // 32):
                rows = pl.ds(r0 + 32 * s, 32)
                e = jnp.exp2(raw[rows, cols] - tall(peak, 4))
                ec[rows, cols] = e
                add = sublanes(e, jnp.add)
                total = add if total is None else total + add
            cmax[part, q, :, cols] = peak
            csum[part, q, :, cols] = total

    def tiles(first, last, strip):
        def body(q, carry):
            tile(q, strip, *STRIPS[strip])
            return carry

        lax.fori_loop(first, last, body, 0)

    s1_send()
    for second in range(2):
        for sign in both:
            z_move(sign, 1, second)
    c_move(0)
    t1_send(0)
    s1_recv()
    z_step(1, 0)
    t1_recv(0)
    z_step(1, 1)
    for sign in both:
        c_move(sign)
    s2_recv()
    z_step(2, 0)
    t1_recv(1)
    z_step(2, 1)
    for sign in both:
        c_move(2 * sign)
    t1_recv(2)
    c_come(0)
    tiles(0, 1, 0)
    z_step(3, 0)
    tiles(1, 2, 0)
    t1_recv(3)
    z_step(3, 1)
    for sign in both:
        c_move(3 * sign)
    tiles(2, 3, 0)
    c_come(1)
    tiles(0, 3, 1)
    z_step(4, 0)
    c_move(4)
    t2_recv()
    tile(3, 0, *LAST[0])
    c_come(2)
    tiles(0, 3, 2)
    tile(3, 1, *LAST[1])

    for part in range(2):
        high = jnp.max(cmax[part], axis=0)
        high = jnp.max(high, axis=0, keepdims=True)
        total = jnp.sum(csum[part] * jnp.exp2(cmax[part] - high[None]), axis=0)
        lse = high + jnp.log2(jnp.sum(total, axis=0, keepdims=True))
        for dz in range(8):
            k = SLOT[dz]
            cst[pl.ds(part * 8 + (z + dz) % 8, 1), :] = lse[:, 128 * k:128 * k + 128]
    for dz, dc in column:
        i, dev = column_peer(dz, dc)
        send(cst, cst_in.at[me_c], cx_s, cx_r, dev)

    for part in range(2):
        for k in range(8):
            rows = pl.ds(128 * k, 128)
            strips = range(3 if k < 6 else 2)
            m = [rmax[part, s, rows, :] for s in strips]
            high = functools.reduce(jnp.maximum, m)
            total = functools.reduce(jnp.add, [rsum[part, s, rows, :] * jnp.exp2(m[s] - high) for s in strips])
            high, total = high.T, total.T
            peak = jnp.max(high, axis=0, keepdims=True)
            lse = peak + jnp.log2(jnp.sum(total * jnp.exp2(high - peak), axis=0, keepdims=True))
            for h, a, b, r in UNITS:
                if r // 128 == k:
                    o = r % 128
                    rel[pl.ds(part * 8 + h * 4 + b, 1), pl.ds(32 * a, 32)] = lse[:, o:o + 32]
        v = rel[pl.ds(part * 8, 8), :]
        v = (pltpu.roll(v, 32 * x, axis=1), pltpu.roll(v, 32 * y, axis=1))
        for h in range(2):
            for b in range(4):
                k = h * 4 + b
                rst[pl.ds(part * 8 + h * 4 + (b + (y, x)[h]) % 4, 1), :] = v[h][k:k + 1]
    for dx, dy in plane:
        i, dev = plane_peer(dx, dy)
        send(rst, rst_in.at[me_p], rx_s, rx_r, dev)
    cst_in[me_c] = cst[...]
    rst_in[me_p] = rst[...]

    def total_lse(v):
        m = jnp.max(v, axis=0)
        return m + jnp.log2(jnp.sum(jnp.exp2(v - m[None]), axis=0))

    half = 0.5 * sscale[0]
    arrived(cst_in.at[pl.ds(0, 15)], cx_s, cx_r)
    col = total_lse(cst_in[...])
    call[...] = col
    for part in range(2):
        lse = [None] * 8
        for dz in range(8):
            lse[SLOT[dz]] = call[pl.ds(part * 8 + (z + dz) % 8, 1), :]
        cmax[part] = half * jnp.exp2(cmax[part] - jnp.concatenate(lse, axis=1)[None])
    arrived(rst_in.at[pl.ds(0, 15)], rx_s, rx_r)
    row = total_lse(rst_in[...])
    rall[...] = row
    for part in range(2):
        for h in range(2):
            for b in range(4):
                rel[pl.ds(part * 8 + h * 4 + b, 1), :] = rall[pl.ds(part * 8 + h * 4 + (b + (y, x)[h]) % 4, 1), :]
        v = rel[pl.ds(part * 8, 8), :]
        v = (pltpu.roll(v, 128 - 32 * x, axis=1), pltpu.roll(v, 128 - 32 * y, axis=1))
        for k in range(8):
            mine = sorted((r, h, a, b) for h, a, b, r in UNITS if r // 128 == k)
            lse = jnp.concatenate(
                [v[h][h * 4 + b:h * 4 + b + 1, 32 * a:32 * a + 32] for _, h, a, b in mine], axis=1
            )
            lse = jnp.broadcast_to(lse, (128, 128)).T
            rows = pl.ds(128 * k, 128)
            for s in range(3 if k < 6 else 2):
                rmax[part, s, rows, :] = half * jnp.exp2(rmax[part, s, rows, :] - lse)

    def pass2(c0, n, head, last, carry):
        cols = pl.ds(c0, n)
        k = n // 128

        def body(s, carry, strip):
            loss_acc, scale_acc = carry
            rows = pl.ds(pl.multiple_of(s * 32, 32), 32)
            q = s // (CHUNK // 32)
            v = vs[rows, cols]
            teach = ert[rows, cols] * wide(rmax[0, strip, rows, :], k) + ect[rows, cols] * tall(cmax[0, q, :, cols], 4)
            stud = ers[rows, cols] * wide(rmax[1, strip, rows, :], k) + ecs[rows, cols] * tall(cmax[1, q, :, cols], 4)
            differ = stud - teach
            wts[rows, cols] = differ.astype(jnp.bfloat16)
            loss_acc = loss_acc + lanes(sublanes(teach * v, jnp.add), jnp.add)
            scale_acc = scale_acc + lanes(sublanes(differ * v, jnp.add), jnp.add)
            return loss_acc, scale_acc

        carry = lax.fori_loop(0, 24, functools.partial(body, strip=head), carry, unroll=4)
        return lax.fori_loop(24, 32, functools.partial(body, strip=last), carry, unroll=4)

    def text_parts(q):
        v = lax.dot_general(
            wts[:, 256 * q:256 * q + 256], img[:, TW:], TN, preferred_element_type=jnp.float32
        )
        pair = pl.ds(2 * q, 2)
        gt_all[pair] = v.reshape(2, 2, ROWS, SW)
        send(gt_all.at[pair, sib], gt_sib.at[pair], sb_s, sb_r.at[q], other)

    def text_both(q):
        arrived(gt_sib.at[pl.ds(2 * q, 2)], sb_s, sb_r.at[q])

    def own_part(dz, q):
        rows = pl.ds(32 * q, 32)
        return gt_all[SLOT[dz % 8], c, rows, :] + gt_sib[SLOT[dz % 8], rows, :]

    def chain_ref(ref, sign, s, q):
        return ref.at[s * 2 + (sign > 0), pl.ds(32 * q, 32)]

    def chain_wait(s, q):
        arrived(gt_in.at[0], gt_s, gt_r.at[s * 2 + q])

    def chain_part(sign, s, q):
        return chain_ref(gt_in, sign, s, q)[...].astype(jnp.float32)

    def chain_send(sign, s, q):
        v = own_part(sign * (3 - s), q)
        if s > 0:
            v = v + chain_part(sign, s - 1, q)
        chain_ref(gt_snd, sign, s, q)[...] = v.astype(jnp.bfloat16)
        send(chain_ref(gt_snd, sign, s, q), chain_ref(gt_in, sign, s, q), gt_s, gt_r.at[s * 2 + q], up(sign))

    def chain_step(s):
        for q in range(2):
            chain_wait(s - 1, q)
            for sign in both:
                chain_send(sign, s, q)

    def far_send():
        for q in range(2):
            gt_snd[6, pl.ds(32 * q, 32)] = own_part(4, q).astype(jnp.bfloat16)
        send(gt_snd.at[6], gt_in.at[6], gt_s, gt_r.at[6], up(4))

    def image_parts(q):
        v = jnp.dot(
            wts[pl.ds(256 * q, 256), :], txt[:, :, :, TW:].reshape(TILE, SW), preferred_element_type=jnp.float32
        )
        for h, a, b, r in UNITS:
            if r // 256 == q:
                o = r % 256
                if b == 0:
                    gi_own[h, a] = v[o:o + 32]
                else:
                    gi_snd[h, b, a] = v[o:o + 32].astype(jnp.bfloat16)

    pieces = ((2, 2), (1, 1), (0, 1))

    def stage1_send(b, p):
        for h in range(2):
            part = pl.ds(*pieces[p])
            send(gi_snd.at[h, b, part], gi_in.at[h, 4 - b, part], g1_s, g1_r.at[h * 3 + p], along(h, 1, b))

    def stage1_sum(h, p):
        first_a, count = pieces[p]
        arrived(gi_in.at[h, pl.ds(1, 3), pl.ds(first_a, count)], g1_s, g1_r.at[h * 3 + p])
        for a in range(first_a, first_a + count):
            v = gi_own[h, a] + gi_in[h, 1, a].astype(jnp.float32)
            v = v + gi_in[h, 2, a].astype(jnp.float32) + gi_in[h, 3, a].astype(jnp.float32)
            if a == 0:
                gi_mid[h] = v
            else:
                g2_snd[h, a] = v.astype(jnp.bfloat16)
                send(g2_snd.at[h, a], g2_in.at[h, 4 - a], g2_s, g2_r.at[h], along(h, 0, a))

    def stage2_sum(h):
        arrived(g2_in.at[h, pl.ds(1, 3)], g2_s, g2_r.at[h])
        v = gi_mid[h]
        for a in range(1, 4):
            v = v + g2_in[h, a].astype(jnp.float32)
        gi_out[pl.ds(32 * h, 32), :] = v

    def scalar_send(level, peers, peer, me):
        for p in peers:
            i, dev = peer(*p)
            send(sc_snd.at[level], sc_in.at[level, me], sc_s, sc_r.at[level], dev)

    def scalar_sum(level, me):
        arrived(sc_in.at[level, pl.ds(0, 15)], sc_s, sc_r.at[level])
        sc_in[level, me] = sc_snd[level]
        return jnp.sum(sc_in[level], axis=0)

    in_plane = (plane, plane_peer, me_p)
    in_column = (column, column_peer, me_c)

    zero = jnp.zeros((8, 128), jnp.float32)
    accs = pass2(768, 256, 2, 1, (zero, zero))
    text_parts(3)
    accs = pass2(512, 256, 1, 1, accs)
    text_parts(2)
    loss_acc, scale_acc = pass2(0, 512, 0, 0, accs)

    back = LN2 / half
    loss_acc = (row[8:, :] + col[8:, :]) * (LN2 / 16.0) - loss_acc * back
    sc_snd[0, pl.ds(0, 1), :] = jnp.sum(loss_acc, axis=0, keepdims=True)
    sc_snd[0, pl.ds(1, 1), :] = jnp.sum(scale_acc * back, axis=0, keepdims=True)
    scalar_send(0, *in_plane)

    text_both(3)
    for q in range(2):
        chain_send(-1, 0, q)
    image_parts(3)
    for p in range(3):
        stage1_send(2, p)
    image_parts(1)
    image_parts(2)
    for p in range(3):
        for b in (1, 3):
            stage1_send(b, p)
    text_both(2)
    for q in range(2):
        chain_send(1, 0, q)

    text_parts(1)
    text_parts(0)
    image_parts(0)
    sc_snd[1] = scalar_sum(0, me_p)
    scalar_send(1, *in_column)
    far_send()
    text_both(1)
    chain_step(1)
    for h in range(2):
        stage1_sum(h, 0)
    text_both(0)
    chain_step(2)
    for h in range(2):
        stage1_sum(h, 1)
    arrived(gt_in.at[6], gt_s, gt_r.at[6])
    for h in range(2):
        stage1_sum(h, 2)
    total = scalar_sum(1, me_c)
    for q in range(2):
        rows = pl.ds(32 * q, 32)
        chain_wait(2, q)
        v = own_part(0, q) + gt_in[6, rows, :].astype(jnp.float32)
        gt_out[rows, :] = v + chain_part(1, 2, q) + chain_part(-1, 2, q)
    for h in range(2):
        stage2_sum(h)
    pairs = 2.0 * TILE * 16
    sums_out[pl.ds(0, 1), :] = total[:1] / pairs
    sums_out[pl.ds(1, 1), :] = total[1:] / (pairs * sscale[0])
    all_sent(img.at[pl.ds(0, 960)], ps_s, ps_r.at[0])
    all_sent(txt.at[pl.ds(0, 7), 0], zs_s, zs_r.at[0])
    all_sent(txt.at[:, 0], cs_s, cs_r.at[0])
    all_sent(rst_in.at[pl.ds(0, 15)], rx_s, rx_r)
    all_sent(cst_in.at[pl.ds(0, 15)], cx_s, cx_r)
    all_sent(gi_in.at[:, pl.ds(0, 3)], g1_s, g1_r.at[0])
    all_sent(g2_in.at[:, pl.ds(0, 3)], g2_s, g2_r.at[0])
    all_sent(gt_sib, sb_s, sb_r.at[0])
    all_sent(gt_in.at[pl.ds(0, 7)], gt_s, gt_r.at[0])
    all_sent(sc_in.at[:, pl.ds(0, 15)], sc_s, sc_r.at[0])


def finish(gi, gt, sums, gi_out, gt_out, loss_out, gs_out):
    gi_out[...] = gi[...]
    gt_out[...] = gt[...]
    loss_out[0] = jnp.sum(sums[pl.ds(0, 1), :])
    gs_out[0] = jnp.sum(sums[pl.ds(1, 1), :])


def shards(*args):
    f32, bf16 = jnp.float32, jnp.bfloat16
    anyw = pl.BlockSpec(memory_space=pl.ANY)
    vmem = pl.BlockSpec(memory_space=pltpu.VMEM)
    smem = pl.BlockSpec(memory_space=pltpu.SMEM)
    sem = pltpu.SemaphoreType.DMA
    V = pltpu.VMEM
    rows = jax.ShapeDtypeStruct((ROWS, SW), f32)
    one = jax.ShapeDtypeStruct((1,), f32)
    sums = pl.pallas_call(
        kernel,
        out_shape=(rows, rows, jax.ShapeDtypeStruct((2, 128), f32)),
        in_specs=[anyw] * 4 + [smem] * 2,
        out_specs=(vmem, vmem, vmem),
        scratch_shapes=[
            V((TILE, W), bf16),
            V((NZ, 2, ROWS, W), bf16),
            V((TILE, TILE), f32),
            V((TILE, TILE), f32),
            V((TILE, TILE), f32),
            V((TILE, TILE), f32),
            V((TILE, TILE), f32),
            V((TILE, TILE), f32),
            V((TILE, TILE), bf16),
            V((2, 3, TILE, 128), f32),
            V((2, 3, TILE, 128), f32),
            V((2, 4, 8, TILE), f32),
            V((2, 4, 8, TILE), f32),
            V((16, 128), f32),
            V((16, 128), f32),
            V((16, 128), f32),
            V((16, 128), f32),
            V((16, 128), f32),
            V((16, 16, 128), f32),
            V((16, 16, 128), f32),
            V((2, 4, 32, SW), f32),
            V((2, 32, SW), f32),
            V((2, 4, 4, 32, SW), bf16),
            V((2, 4, 4, 32, SW), bf16),
            V((2, 4, 32, SW), bf16),
            V((2, 4, 32, SW), bf16),
            V((8, 2, ROWS, SW), f32),
            V((8, ROWS, SW), f32),
            V((8, ROWS, SW), bf16),
            V((8, ROWS, SW), bf16),
            V((2, 2, 128), f32),
            V((2, 16, 2, 128), f32),
            sem,
            sem, sem((7,)),
            sem, sem((7,)),
            sem, sem((3,)),
            sem, sem,
            sem, sem,
            sem, sem((6,)),
            sem, sem((2,)),
            sem, sem((4,)),
            sem, sem((7,)),
            sem, sem((2,)),
        ],
        compiler_params=pltpu.CompilerParams(
            collective_id=0, has_side_effects=True, vmem_limit_bytes=60 * 1024 * 1024
        ),
    )(*args)
    return tuple(pl.pallas_call(
        finish,
        out_shape=(rows, rows, one, one),
        in_specs=[vmem] * 3,
        out_specs=(vmem, vmem, smem, smem),
    )(*sums))


def solution(mesh):
    return jax.shard_map(
        shards,
        mesh=mesh,
        in_specs=(
            P(("grp", "dev"), None),
            P(("grp", "dev"), None),
            P(("grp", "dev"), None),
            P(("grp", "dev"), None),
            P(),
            P(),
        ),
        out_specs=(P(("grp", "dev"), None), P(("grp", "dev"), None), P(), P()),
        check_vma=False,
    )
```

```python
import functools

import jax
import jax.numpy as jnp
from jax import lax
from jax.experimental import pallas as pl
from jax.experimental.pallas import tpu as pltpu
from jax.sharding import PartitionSpec as P

NX, NY, NZ = 4, 4, 8
ROWS = 64
TW, SW = 1280, 512
W = TW + SW
TILE = 1024
CHUNK = 256
LOG2E = 1.4426950408889634
LN2 = 0.6931471805599453
MESH = pl.DeviceIdType.MESH
NT = (((1,), (1,)), ((), ()))
TN = (((0,), (0,)), ((), ()))

A_OF = (0, 3, 1, 2)
SLOT = (0, 1, 3, 5, 7, 6, 4, 2)
STRIPS = ((0, 512), (512, 256), (768, 256))
LAST = ((0, 512), (512, 512))


def row_unit(h, a, b):
    k = A_OF.index(a)
    if b == 0:
        return 128 * h + 32 * a
    if b == 2:
        return 768 + 64 * k + 32 * h
    return 256 + 128 * k + (0 if b == 3 else 64) + 32 * h


UNITS = tuple((h, a, b, row_unit(h, a, b)) for h in range(2) for a in range(4) for b in range(4))


def lanes(v, op):
    return functools.reduce(op, [v[:, 128 * k:128 * k + 128] for k in range(v.shape[1] // 128)])


def sublanes(v, op):
    return functools.reduce(op, [v[8 * k:8 * k + 8] for k in range(v.shape[0] // 8)])


def wide(v, n):
    return jnp.concatenate([v] * n, axis=1)


def tall(v, n):
    return jnp.concatenate([v] * n, axis=0)


def kernel(
    ti, tt, si, st, tscale, sscale,
    gi_out, gt_out, sums_out,
    img, txt, vt, vs, ert, ect, ers, ecs, wts,
    rmax, rsum, cmax, csum, rel, rst, cst, rall, call, rst_in, cst_in,
    gi_own, gi_mid, gi_snd, gi_in, g2_snd, g2_in, gt_all, gt_sib, gt_snd, gt_in,
    sc_snd, sc_in,
    loc_sem, ps_s, ps_r, zs_s, zs_r, cs_s, cs_r,
    rx_s, rx_r, cx_s, cx_r, g1_s, g1_r, g2_s, g2_r, sb_s, sb_r, gt_s, gt_r,
    sc_s, sc_r,
):
    g, d = lax.axis_index("grp"), lax.axis_index("dev")
    x, y, z, c = g % 4, d // 4, ((d // 2) % 2) * 4 + g // 4, d % 2
    me_p, me_c = y * 4 + x, z * 2 + c
    sib = 1 - c

    def at(xx, yy, zz, cc):
        return ((zz % 4) * 4 + xx, yy * 4 + (zz // 4) * 2 + cc)

    plane = [(dx, dy) for dy in range(NY) for dx in range(NX) if (dx, dy) != (0, 0)]
    column = [(dz, dc) for dz in range(NZ) for dc in range(2) if (dz, dc) != (0, 0)]

    def plane_peer(dx, dy):
        px, py = (x + dx) % NX, (y + dy) % NY
        return py * 4 + px, at(px, py, z, c)

    def column_peer(dz, dc):
        pz, pc = (z + dz) % NZ, (c + dc) % 2
        return pz * 2 + pc, at(x, y, pz, pc)

    def along(h, axis, step):
        if (h + axis) % 2 == 0:
            return at((x + step) % NX, y, z, c)
        return at(x, (y + step) % NY, z, c)

    def up(step):
        return at(x, y, (z + step) % NZ, c)

    other = at(x, y, z, sib)

    local = []

    def bring(src, dst):
        cp = pltpu.make_async_copy(src, dst, loc_sem)
        cp.start()
        local.append(cp)

    for h in range(2):
        r = row_unit(h, 0, 0)
        bring(ti.at[pl.ds(32 * h, 32)], img.at[pl.ds(r, 32), pl.ds(0, TW)])
        bring(si.at[pl.ds(32 * h, 32)], img.at[pl.ds(r, 32), pl.ds(TW, SW)])
    bring(tt, txt.at[0, c, :, pl.ds(0, TW)])
    bring(st, txt.at[0, c, :, pl.ds(TW, SW)])

    barrier = pltpu.get_barrier_semaphore()
    near = [along(0, axis, step) for axis in range(2) for step in (1, -1)] + [up(1), up(-1), other]
    for dev in near:
        pl.semaphore_signal(barrier, inc=1, device_id=dev, device_id_type=MESH)
    pltpu.make_async_copy(img.at[pl.ds(0, 2 * ROWS)], img.at[pl.ds(0, 2 * ROWS)], loc_sem).wait()
    pl.semaphore_wait(barrier, len(near))

    def remote(src, dst, ssem, rsem, dev):
        return pltpu.make_async_remote_copy(
            src_ref=src, dst_ref=dst, send_sem=ssem, recv_sem=rsem, device_id=dev, device_id_type=MESH
        )

    def send(src, dst, ssem, rsem, dev):
        remote(src, dst, ssem, rsem, dev).start()

    def arrived(like, ssem, rsem):
        remote(like, like, ssem, rsem, other).wait_recv()

    def all_sent(like, ssem, rsem):
        remote(like, like, ssem, rsem, other).wait_send()

    both = (1, -1)

    def unit(h, a, b, r0=0, n=32):
        return img.at[pl.ds(row_unit(h, a % 4, b % 4) + r0, n)]

    def psend(h, i, sign, src, dst, axis):
        send(src, dst, ps_s, ps_r.at[i], along(h, axis, sign))

    def pwait(i, n):
        arrived(img.at[pl.ds(0, n)], ps_s, ps_r.at[i])

    def half_of(sign):
        return (0 if sign > 0 else 16), 16

    hs = [(h, sign) for h in range(2) for sign in both]

    def s1_send():
        for h, sign in hs:
            psend(h, 0, sign, unit(h, 0, 0), unit(h, -sign, 0), 0)

    def s1_recv():
        pwait(0, 128)
        for h, sign in hs:
            psend(h, 1, sign, unit(h, -sign, 0, *half_of(sign)), unit(h, 2, 0, *half_of(sign)), 0)
        t1_send(1)
        t1_send(2)

    def s2_recv():
        pwait(1, 64)
        t1_send(3)

    def t1_send(k):
        for h, sign in hs:
            psend(h, 2 + k, sign, unit(h, A_OF[k], 0), unit(h, A_OF[k], -sign), 1)

    def t1_recv(k):
        pwait(2 + k, 128)
        for h, sign in hs:
            psend(h, 6, sign, unit(h, A_OF[k], -sign, *half_of(sign)), unit(h, A_OF[k], 2, *half_of(sign)), 1)

    def t2_recv():
        pwait(6, 256)

    def zpart(dz, q):
        return txt.at[SLOT[dz % 8], c, pl.ds(32 * q, 32)]

    def first_half(sign):
        return 0 if sign > 0 else 1

    def z_move(sign, s, second):
        q = first_half(sign) ^ second
        send(zpart(-sign * (s - 1), q), zpart(-sign * s, q), zs_s, zs_r.at[(s - 1) * 2 + second], up(sign))

    def z_step(s, second):
        arrived(txt.at[0, 0], zs_s, zs_r.at[(s - 1) * 2 + second])
        for sign in both:
            if s < 3 or (s == 3 and not second):
                z_move(sign, s + 1, second)

    groups = ((0, 4), (4, 2), (6, 2))

    def c_move(dz):
        k = SLOT[dz % 8]
        i = (k >= 4) + (k >= 6)
        send(txt.at[k, c], txt.at[k, c], cs_s, cs_r.at[i], other)

    def c_come(i):
        arrived(txt.at[pl.ds(*groups[i]), sib], cs_s, cs_r.at[i])

    lt, ls = tscale[0] * LOG2E, sscale[0] * LOG2E
    parts = ((0, TW, lt, vt, ert, ect), (TW, W, ls, vs, ers, ecs))

    def tile(q, strip, c0, n):
        r0 = q * CHUNK
        cols = pl.ds(c0, n)
        blocks = pl.ds(c0 // 128, n // 128)
        for part, (lo, hi, scale, raw, er, ec) in enumerate(parts):
            raw[pl.ds(r0, CHUNK), cols] = scale * lax.dot_general(
                img[pl.ds(r0, CHUNK), lo:hi],
                txt[blocks, :, :, lo:hi].reshape(n, hi - lo),
                NT,
                preferred_element_type=jnp.float32,
            )
            peak = None
            for s in range(CHUNK // 32):
                rows = pl.ds(r0 + 32 * s, 32)
                v = raw[rows, cols]
                m = lanes(v, jnp.maximum)
                e = jnp.exp2(v - wide(m, n // 128))
                er[rows, cols] = e
                rmax[part, strip, rows, :] = m
                rsum[part, strip, rows, :] = lanes(e, jnp.add)
                high = sublanes(v, jnp.maximum)
                peak = high if peak is None else jnp.maximum(peak, high)
            total = None
            for s in range(CHUNK // 32):
                rows = pl.ds(r0 + 32 * s, 32)
                e = jnp.exp2(raw[rows, cols] - tall(peak, 4))
                ec[rows, cols] = e
                add = sublanes(e, jnp.add)
                total = add if total is None else total + add
            cmax[part, q, :, cols] = peak
            csum[part, q, :, cols] = total

    def tiles(first, last, strip):
        def body(q, carry):
            tile(q, strip, *STRIPS[strip])
            return carry

        lax.fori_loop(first, last, body, 0)

    s1_send()
    for second in range(2):
        for sign in both:
            z_move(sign, 1, second)
    c_move(0)
    t1_send(0)
    s1_recv()
    z_step(1, 0)
    t1_recv(0)
    z_step(1, 1)
    for sign in both:
        c_move(sign)
    s2_recv()
    z_step(2, 0)
    t1_recv(1)
    z_step(2, 1)
    for sign in both:
        c_move(2 * sign)
    t1_recv(2)
    c_come(0)
    tiles(0, 1, 0)
    z_step(3, 0)
    tiles(1, 2, 0)
    t1_recv(3)
    z_step(3, 1)
    for sign in both:
        c_move(3 * sign)
    tiles(2, 3, 0)
    c_come(1)
    tiles(0, 3, 1)
    z_step(4, 0)
    c_move(4)
    t2_recv()
    tile(3, 0, *LAST[0])
    c_come(2)
    tiles(0, 3, 2)
    tile(3, 1, *LAST[1])

    for part in range(2):
        high = jnp.max(cmax[part], axis=0)
        high = jnp.max(high, axis=0, keepdims=True)
        total = jnp.sum(csum[part] * jnp.exp2(cmax[part] - high[None]), axis=0)
        lse = high + jnp.log2(jnp.sum(total, axis=0, keepdims=True))
        for dz in range(8):
            k = SLOT[dz]
            cst[pl.ds(part * 8 + (z + dz) % 8, 1), :] = lse[:, 128 * k:128 * k + 128]
    for dz, dc in column:
        i, dev = column_peer(dz, dc)
        send(cst, cst_in.at[me_c], cx_s, cx_r, dev)

    for part in range(2):
        for k in range(8):
            rows = pl.ds(128 * k, 128)
            strips = range(3 if k < 6 else 2)
            m = [rmax[part, s, rows, :] for s in strips]
            high = functools.reduce(jnp.maximum, m)
            total = functools.reduce(jnp.add, [rsum[part, s, rows, :] * jnp.exp2(m[s] - high) for s in strips])
            high, total = high.T, total.T
            peak = jnp.max(high, axis=0, keepdims=True)
            lse = peak + jnp.log2(jnp.sum(total * jnp.exp2(high - peak), axis=0, keepdims=True))
            for h, a, b, r in UNITS:
                if r // 128 == k:
                    o = r % 128
                    rel[pl.ds(part * 8 + h * 4 + b, 1), pl.ds(32 * a, 32)] = lse[:, o:o + 32]
        v = rel[pl.ds(part * 8, 8), :]
        v = (pltpu.roll(v, 32 * x, axis=1), pltpu.roll(v, 32 * y, axis=1))
        for h in range(2):
            for b in range(4):
                k = h * 4 + b
                rst[pl.ds(part * 8 + h * 4 + (b + (y, x)[h]) % 4, 1), :] = v[h][k:k + 1]
    for dx, dy in plane:
        i, dev = plane_peer(dx, dy)
        send(rst, rst_in.at[me_p], rx_s, rx_r, dev)
    cst_in[me_c] = cst[...]
    rst_in[me_p] = rst[...]

    def total_lse(v):
        m = jnp.max(v, axis=0)
        return m + jnp.log2(jnp.sum(jnp.exp2(v - m[None]), axis=0))

    half = 0.5 * sscale[0]
    arrived(cst_in.at[pl.ds(0, 15)], cx_s, cx_r)
    col = total_lse(cst_in[...])
    call[...] = col
    for part in range(2):
        lse = [None] * 8
        for dz in range(8):
            lse[SLOT[dz]] = call[pl.ds(part * 8 + (z + dz) % 8, 1), :]
        cmax[part] = half * jnp.exp2(cmax[part] - jnp.concatenate(lse, axis=1)[None])
    arrived(rst_in.at[pl.ds(0, 15)], rx_s, rx_r)
    row = total_lse(rst_in[...])
    rall[...] = row
    for part in range(2):
        for h in range(2):
            for b in range(4):
                rel[pl.ds(part * 8 + h * 4 + b, 1), :] = rall[pl.ds(part * 8 + h * 4 + (b + (y, x)[h]) % 4, 1), :]
        v = rel[pl.ds(part * 8, 8), :]
        v = (pltpu.roll(v, 128 - 32 * x, axis=1), pltpu.roll(v, 128 - 32 * y, axis=1))
        for k in range(8):
            mine = sorted((r, h, a, b) for h, a, b, r in UNITS if r // 128 == k)
            lse = jnp.concatenate(
                [v[h][h * 4 + b:h * 4 + b + 1, 32 * a:32 * a + 32] for _, h, a, b in mine], axis=1
            )
            lse = jnp.broadcast_to(lse, (128, 128)).T
            rows = pl.ds(128 * k, 128)
            for s in range(3 if k < 6 else 2):
                rmax[part, s, rows, :] = half * jnp.exp2(rmax[part, s, rows, :] - lse)

    def pass2(pieces, carry):
        def body(s, carry, group):
            loss_acc, scale_acc = carry
            rows = pl.ds(pl.multiple_of(s * 32, 32), 32)
            q = s // (CHUNK // 32)
            for c0, n, *strips in pieces:
                cols = pl.ds(c0, n)
                k = n // 128
                strip = strips[group]
                v = vs[rows, cols]
                teach = ert[rows, cols] * wide(rmax[0, strip, rows, :], k) + ect[rows, cols] * tall(cmax[0, q, :, cols], 4)
                stud = ers[rows, cols] * wide(rmax[1, strip, rows, :], k) + ecs[rows, cols] * tall(cmax[1, q, :, cols], 4)
                differ = stud - teach
                wts[rows, cols] = differ.astype(jnp.bfloat16)
                loss_acc = loss_acc + lanes(sublanes(teach * v, jnp.add), jnp.add)
                scale_acc = scale_acc + lanes(sublanes(differ * v, jnp.add), jnp.add)
            return loss_acc, scale_acc

        carry = lax.fori_loop(0, 24, functools.partial(body, group=0), carry, unroll=2)
        return lax.fori_loop(24, 32, functools.partial(body, group=1), carry, unroll=2)

    slots = ((5, 3), (3, 2), (1, 2), (0, 1))

    def text_parts(i):
        k, n = slots[i]
        v = lax.dot_general(
            wts[:, 128 * k:128 * (k + n)], img[:, TW:], TN, preferred_element_type=jnp.float32
        )
        some = pl.ds(k, n)
        gt_all[some] = v.reshape(n, 2, ROWS, SW)
        send(gt_all.at[some, sib], gt_sib.at[some], sb_s, sb_r.at[i], other)

    def text_both(i):
        arrived(gt_sib.at[pl.ds(*slots[i])], sb_s, sb_r.at[i])

    def own_part(dz, q):
        rows = pl.ds(32 * q, 32)
        return gt_all[SLOT[dz % 8], c, rows, :] + gt_sib[SLOT[dz % 8], rows, :]

    def chain_ref(ref, sign, s, q):
        return ref.at[s * 2 + (sign > 0), pl.ds(32 * q, 32)]

    def chain_wait(s, second):
        arrived(gt_in.at[0], gt_s, gt_r.at[s * 2 + second])

    def chain_part(sign, s, q):
        return chain_ref(gt_in, sign, s, q)[...].astype(jnp.float32)

    def chain_send(s, second):
        for sign in both:
            q = first_half(sign) ^ second
            v = own_part(sign * (3 - s), q)
            if s > 0:
                v = v + chain_part(sign, s - 1, q)
            if s == 1 and not second:
                v = v + gt_in[6, pl.ds(32 * q, 32), :].astype(jnp.float32)
            chain_ref(gt_snd, sign, s, q)[...] = v.astype(jnp.bfloat16)
            send(chain_ref(gt_snd, sign, s, q), chain_ref(gt_in, sign, s, q), gt_s, gt_r.at[s * 2 + second], up(sign))

    def far_send():
        for sign in both:
            rows = pl.ds(32 * first_half(sign), 32)
            gt_snd[6, rows] = own_part(4, first_half(sign)).astype(jnp.bfloat16)
            send(gt_snd.at[6, rows], gt_in.at[6, rows], gt_s, gt_r.at[6], up(2 * sign))

    def image_parts(q):
        v = jnp.dot(
            wts[pl.ds(256 * q, 256), :], txt[:, :, :, TW:].reshape(TILE, SW), preferred_element_type=jnp.float32
        )
        for h, a, b, r in UNITS:
            if r // 256 == q:
                o = r % 256
                if b == 0:
                    gi_own[h, a] = v[o:o + 32]
                else:
                    gi_snd[h, b, a] = v[o:o + 32].astype(jnp.bfloat16)

    pieces = ((2, 2), (1, 1), (0, 1))

    def stage1_send(b, p):
        for h in range(2):
            part = pl.ds(*pieces[p])
            send(gi_snd.at[h, b, part], gi_in.at[h, 4 - b, part], g1_s, g1_r.at[h * 3 + p], along(h, 1, b))

    def stage1_sum(h, p):
        first_a, count = pieces[p]
        arrived(gi_in.at[h, pl.ds(1, 3), pl.ds(first_a, count)], g1_s, g1_r.at[h * 3 + p])
        for a in range(first_a, first_a + count):
            v = gi_own[h, a] + gi_in[h, 1, a].astype(jnp.float32)
            v = v + gi_in[h, 2, a].astype(jnp.float32) + gi_in[h, 3, a].astype(jnp.float32)
            if a == 0:
                gi_mid[h] = v
            else:
                g2_snd[h, a] = v.astype(jnp.bfloat16)
                send(g2_snd.at[h, a], g2_in.at[h, 4 - a], g2_s, g2_r.at[h], along(h, 0, a))

    def stage2_sum(h):
        arrived(g2_in.at[h, pl.ds(1, 3)], g2_s, g2_r.at[h])
        v = gi_mid[h]
        for a in range(1, 4):
            v = v + g2_in[h, a].astype(jnp.float32)
        gi_out[pl.ds(32 * h, 32), :] = v

    def scalar_send(level, peers, peer, me):
        for p in peers:
            i, dev = peer(*p)
            send(sc_snd.at[level], sc_in.at[level, me], sc_s, sc_r.at[level], dev)

    def scalar_sum(level, me):
        arrived(sc_in.at[level, pl.ds(0, 15)], sc_s, sc_r.at[level])
        sc_in[level, me] = sc_snd[level]
        return jnp.sum(sc_in[level], axis=0)

    in_plane = (plane, plane_peer, me_p)
    in_column = (column, column_peer, me_c)

    zero = jnp.zeros((8, 128), jnp.float32)
    accs = pass2(((640, 128, 1, 1), (768, 256, 2, 1)), (zero, zero))
    text_parts(0)
    loss_acc, scale_acc = pass2(((512, 128, 1, 1), (0, 512, 0, 0)), accs)

    back = LN2 / half
    loss_acc = (row[8:, :] + col[8:, :]) * (LN2 / 16.0) - loss_acc * back
    sc_snd[0, pl.ds(0, 1), :] = jnp.sum(loss_acc, axis=0, keepdims=True)
    sc_snd[0, pl.ds(1, 1), :] = jnp.sum(scale_acc * back, axis=0, keepdims=True)
    scalar_send(0, *in_plane)

    text_both(0)
    far_send()
    chain_send(0, 1)
    chain_send(0, 0)
    text_parts(1)
    for q in (3, 1, 2):
        image_parts(q)
    for p in range(3):
        for b in (2, 1, 3):
            stage1_send(b, p)
    text_parts(2)
    text_both(1)
    chain_wait(0, 1)
    chain_send(1, 1)
    chain_wait(0, 0)
    arrived(gt_in.at[6], gt_s, gt_r.at[6])
    chain_send(1, 0)
    image_parts(0)
    text_parts(3)
    sc_snd[1] = scalar_sum(0, me_p)
    scalar_send(1, *in_column)
    for h in range(2):
        stage1_sum(h, 0)
    text_both(2)
    for second in (1, 0):
        chain_wait(1, second)
        chain_send(2, second)
    for h in range(2):
        stage1_sum(h, 1)
    for h in range(2):
        stage1_sum(h, 2)
    text_both(3)
    total = scalar_sum(1, me_c)
    for second in (1, 0):
        chain_wait(2, second)
    for q in range(2):
        gt_out[pl.ds(32 * q, 32), :] = own_part(0, q) + chain_part(1, 2, q) + chain_part(-1, 2, q)
    for h in range(2):
        stage2_sum(h)
    pairs = 2.0 * TILE * 16
    sums_out[pl.ds(0, 1), :] = total[:1] / pairs
    sums_out[pl.ds(1, 1), :] = total[1:] / (pairs * sscale[0])
    all_sent(img.at[pl.ds(0, 960)], ps_s, ps_r.at[0])
    all_sent(txt.at[pl.ds(0, 7), 0], zs_s, zs_r.at[0])
    all_sent(txt.at[:, 0], cs_s, cs_r.at[0])
    all_sent(rst_in.at[pl.ds(0, 15)], rx_s, rx_r)
    all_sent(cst_in.at[pl.ds(0, 15)], cx_s, cx_r)
    all_sent(gi_in.at[:, pl.ds(0, 3)], g1_s, g1_r.at[0])
    all_sent(g2_in.at[:, pl.ds(0, 3)], g2_s, g2_r.at[0])
    all_sent(gt_sib, sb_s, sb_r.at[0])
    all_sent(gt_in.at[pl.ds(0, 7)], gt_s, gt_r.at[0])
    all_sent(sc_in.at[:, pl.ds(0, 15)], sc_s, sc_r.at[0])


def finish(gi, gt, sums, gi_out, gt_out, loss_out, gs_out):
    gi_out[...] = gi[...]
    gt_out[...] = gt[...]
    loss_out[0] = jnp.sum(sums[pl.ds(0, 1), :])
    gs_out[0] = jnp.sum(sums[pl.ds(1, 1), :])


def shards(*args):
    f32, bf16 = jnp.float32, jnp.bfloat16
    anyw = pl.BlockSpec(memory_space=pl.ANY)
    vmem = pl.BlockSpec(memory_space=pltpu.VMEM)
    smem = pl.BlockSpec(memory_space=pltpu.SMEM)
    sem = pltpu.SemaphoreType.DMA
    V = pltpu.VMEM
    rows = jax.ShapeDtypeStruct((ROWS, SW), f32)
    one = jax.ShapeDtypeStruct((1,), f32)
    sums = pl.pallas_call(
        kernel,
        out_shape=(rows, rows, jax.ShapeDtypeStruct((2, 128), f32)),
        in_specs=[anyw] * 4 + [smem] * 2,
        out_specs=(vmem, vmem, vmem),
        scratch_shapes=[
            V((TILE, W), bf16),
            V((NZ, 2, ROWS, W), bf16),
            V((TILE, TILE), f32),
            V((TILE, TILE), f32),
            V((TILE, TILE), f32),
            V((TILE, TILE), f32),
            V((TILE, TILE), f32),
            V((TILE, TILE), f32),
            V((TILE, TILE), bf16),
            V((2, 3, TILE, 128), f32),
            V((2, 3, TILE, 128), f32),
            V((2, 4, 8, TILE), f32),
            V((2, 4, 8, TILE), f32),
            V((16, 128), f32),
            V((16, 128), f32),
            V((16, 128), f32),
            V((16, 128), f32),
            V((16, 128), f32),
            V((16, 16, 128), f32),
            V((16, 16, 128), f32),
            V((2, 4, 32, SW), f32),
            V((2, 32, SW), f32),
            V((2, 4, 4, 32, SW), bf16),
            V((2, 4, 4, 32, SW), bf16),
            V((2, 4, 32, SW), bf16),
            V((2, 4, 32, SW), bf16),
            V((8, 2, ROWS, SW), f32),
            V((8, ROWS, SW), f32),
            V((8, ROWS, SW), bf16),
            V((8, ROWS, SW), bf16),
            V((2, 2, 128), f32),
            V((2, 16, 2, 128), f32),
            sem,
            sem, sem((7,)),
            sem, sem((7,)),
            sem, sem((3,)),
            sem, sem,
            sem, sem,
            sem, sem((6,)),
            sem, sem((2,)),
            sem, sem((4,)),
            sem, sem((7,)),
            sem, sem((2,)),
        ],
        compiler_params=pltpu.CompilerParams(
            collective_id=0, has_side_effects=True, vmem_limit_bytes=60 * 1024 * 1024
        ),
    )(*args)
    return tuple(pl.pallas_call(
        finish,
        out_shape=(rows, rows, one, one),
        in_specs=[vmem] * 3,
        out_specs=(vmem, vmem, smem, smem),
    )(*sums))


def solution(mesh):
    return jax.shard_map(
        shards,
        mesh=mesh,
        in_specs=(
            P(("grp", "dev"), None),
            P(("grp", "dev"), None),
            P(("grp", "dev"), None),
            P(("grp", "dev"), None),
            P(),
            P(),
        ),
        out_specs=(P(("grp", "dev"), None), P(("grp", "dev"), None), P(), P()),
        check_vma=False,
    )
```

```python
import functools

import jax
import jax.numpy as jnp
from jax import lax
from jax.experimental import pallas as pl
from jax.experimental.pallas import tpu as pltpu
from jax.sharding import PartitionSpec as P

NX, NY, NZ = 4, 4, 8
ROWS = 64
TW, SW = 1280, 512
W = TW + SW
TILE = 1024
CHUNK = 256
LOG2E = 1.4426950408889634
LN2 = 0.6931471805599453
MESH = pl.DeviceIdType.MESH
NT = (((1,), (1,)), ((), ()))
TN = (((0,), (0,)), ((), ()))

A_OF = (0, 3, 1, 2)
SLOT = (0, 1, 3, 5, 7, 6, 4, 2)
STRIPS = ((0, 512), (512, 256), (768, 256))
LAST = ((0, 512), (512, 512))


def row_unit(h, a, b):
    k = A_OF.index(a)
    if b == 0:
        return 128 * h + 32 * a
    if b == 2:
        return 768 + 64 * k + 32 * h
    return 256 + 128 * k + (0 if b == 3 else 64) + 32 * h


UNITS = tuple((h, a, b, row_unit(h, a, b)) for h in range(2) for a in range(4) for b in range(4))


def lanes(v, op):
    return functools.reduce(op, [v[:, 128 * k:128 * k + 128] for k in range(v.shape[1] // 128)])


def sublanes(v, op):
    return functools.reduce(op, [v[8 * k:8 * k + 8] for k in range(v.shape[0] // 8)])


def wide(v, n):
    return jnp.concatenate([v] * n, axis=1)


def tall(v, n):
    return jnp.concatenate([v] * n, axis=0)


def kernel(
    ti, tt, si, st, tscale, sscale,
    out,
    img, txt, vt, vs, ert, ect, ers, ecs, wts,
    rmax, rsum, cmax, csum, rel, rst, cst, rall, call, rst_in, cst_in,
    gi_own, gi_mid, gi_snd, gi_in, g2_snd, g2_in, gt_all, gt_sib, gt_snd, gt_in,
    sc_snd, sc_in,
    loc_sem, ps_s, ps_r, zs_s, zs_r, cs_s, cs_r,
    rx_s, rx_r, cx_s, cx_r, g1_s, g1_r, g2_s, g2_r, sb_s, sb_r, gt_s, gt_r,
    sc_s, sc_r,
):
    g, d = lax.axis_index("grp"), lax.axis_index("dev")
    x, y, z, c = g % 4, d // 4, ((d // 2) % 2) * 4 + g // 4, d % 2
    me_p, me_c = y * 4 + x, z * 2 + c
    sib = 1 - c

    def at(xx, yy, zz, cc):
        return ((zz % 4) * 4 + xx, yy * 4 + (zz // 4) * 2 + cc)

    plane = [(dx, dy) for dy in range(NY) for dx in range(NX) if (dx, dy) != (0, 0)]
    column = [(dz, dc) for dz in range(NZ) for dc in range(2) if (dz, dc) != (0, 0)]

    def plane_peer(dx, dy):
        px, py = (x + dx) % NX, (y + dy) % NY
        return py * 4 + px, at(px, py, z, c)

    def column_peer(dz, dc):
        pz, pc = (z + dz) % NZ, (c + dc) % 2
        return pz * 2 + pc, at(x, y, pz, pc)

    def along(h, axis, step):
        if (h + axis) % 2 == 0:
            return at((x + step) % NX, y, z, c)
        return at(x, (y + step) % NY, z, c)

    def up(step):
        return at(x, y, (z + step) % NZ, c)

    other = at(x, y, z, sib)

    local = []

    def bring(src, dst):
        cp = pltpu.make_async_copy(src, dst, loc_sem)
        cp.start()
        local.append(cp)

    for h in range(2):
        r = row_unit(h, 0, 0)
        bring(ti.at[pl.ds(32 * h, 32)], img.at[pl.ds(r, 32), pl.ds(0, TW)])
        bring(si.at[pl.ds(32 * h, 32)], img.at[pl.ds(r, 32), pl.ds(TW, SW)])
    bring(tt, txt.at[0, c, :, pl.ds(0, TW)])
    bring(st, txt.at[0, c, :, pl.ds(TW, SW)])

    barrier = pltpu.get_barrier_semaphore()
    near = [along(0, axis, step) for axis in range(2) for step in (1, -1)] + [up(1), up(-1), other]
    for dev in near:
        pl.semaphore_signal(barrier, inc=1, device_id=dev, device_id_type=MESH)
    pltpu.make_async_copy(img.at[pl.ds(0, 2 * ROWS)], img.at[pl.ds(0, 2 * ROWS)], loc_sem).wait()
    pl.semaphore_wait(barrier, len(near))

    def remote(src, dst, ssem, rsem, dev):
        return pltpu.make_async_remote_copy(
            src_ref=src, dst_ref=dst, send_sem=ssem, recv_sem=rsem, device_id=dev, device_id_type=MESH
        )

    def send(src, dst, ssem, rsem, dev):
        remote(src, dst, ssem, rsem, dev).start()

    def arrived(like, ssem, rsem):
        remote(like, like, ssem, rsem, other).wait_recv()

    def all_sent(like, ssem, rsem):
        remote(like, like, ssem, rsem, other).wait_send()

    both = (1, -1)

    def unit(h, a, b, r0=0, n=32):
        return img.at[pl.ds(row_unit(h, a % 4, b % 4) + r0, n)]

    def psend(h, i, sign, src, dst, axis):
        send(src, dst, ps_s, ps_r.at[i], along(h, axis, sign))

    def pwait(i, n):
        arrived(img.at[pl.ds(0, n)], ps_s, ps_r.at[i])

    def half_of(sign):
        return (0 if sign > 0 else 16), 16

    hs = [(h, sign) for h in range(2) for sign in both]

    def s1_send():
        for h, sign in hs:
            psend(h, 0, sign, unit(h, 0, 0), unit(h, -sign, 0), 0)

    def s1_recv():
        pwait(0, 128)
        for h, sign in hs:
            psend(h, 1, sign, unit(h, -sign, 0, *half_of(sign)), unit(h, 2, 0, *half_of(sign)), 0)
        t1_send(1)
        t1_send(2)

    def s2_recv():
        pwait(1, 64)
        t1_send(3)

    def t1_send(k):
        for h, sign in hs:
            psend(h, 2 + k, sign, unit(h, A_OF[k], 0), unit(h, A_OF[k], -sign), 1)

    def t1_recv(k):
        pwait(2 + k, 128)
        for h, sign in hs:
            psend(h, 6, sign, unit(h, A_OF[k], -sign, *half_of(sign)), unit(h, A_OF[k], 2, *half_of(sign)), 1)

    def t2_recv():
        pwait(6, 256)

    def zpart(dz, q):
        return txt.at[SLOT[dz % 8], c, pl.ds(32 * q, 32)]

    def first_half(sign):
        return 0 if sign > 0 else 1

    def z_move(sign, s, second):
        q = first_half(sign) ^ second
        send(zpart(-sign * (s - 1), q), zpart(-sign * s, q), zs_s, zs_r.at[(s - 1) * 2 + second], up(sign))

    def z_step(s, second):
        arrived(txt.at[0, 0], zs_s, zs_r.at[(s - 1) * 2 + second])
        for sign in both:
            if s < 3 or (s == 3 and not second):
                z_move(sign, s + 1, second)

    groups = ((0, 4), (4, 2), (6, 2))

    def c_move(dz):
        k = SLOT[dz % 8]
        i = (k >= 4) + (k >= 6)
        send(txt.at[k, c], txt.at[k, c], cs_s, cs_r.at[i], other)

    def c_come(i):
        arrived(txt.at[pl.ds(*groups[i]), sib], cs_s, cs_r.at[i])

    lt, ls = tscale[0] * LOG2E, sscale[0] * LOG2E
    parts = ((0, TW, lt, vt, ert, ect), (TW, W, ls, vs, ers, ecs))

    def tile(q, strip, c0, n, count=1):
        cols = pl.ds(c0, n)
        blocks = pl.ds(c0 // 128, n // 128)
        for part, (lo, hi, scale, raw, er, ec) in enumerate(parts):
            all_rows = pl.ds(q * CHUNK, count * CHUNK)
            raw[all_rows, cols] = scale * lax.dot_general(
                img[all_rows, lo:hi],
                txt[blocks, :, :, lo:hi].reshape(n, hi - lo),
                NT,
                preferred_element_type=jnp.float32,
            )
            for g in range(count):
                r0 = (q + g) * CHUNK
                peak = None
                for s in range(CHUNK // 32):
                    rows = pl.ds(r0 + 32 * s, 32)
                    v = raw[rows, cols]
                    m = lanes(v, jnp.maximum)
                    e = jnp.exp2(v - wide(m, n // 128))
                    er[rows, cols] = e
                    rmax[part, strip, rows, :] = m
                    rsum[part, strip, rows, :] = lanes(e, jnp.add)
                    high = sublanes(v, jnp.maximum)
                    peak = high if peak is None else jnp.maximum(peak, high)
                total = None
                for s in range(CHUNK // 32):
                    rows = pl.ds(r0 + 32 * s, 32)
                    e = jnp.exp2(raw[rows, cols] - tall(peak, 4))
                    ec[rows, cols] = e
                    add = sublanes(e, jnp.add)
                    total = add if total is None else total + add
                cmax[part, q + g, :, cols] = peak
                csum[part, q + g, :, cols] = total

    def tiles(first, last, strip):
        def body(q, carry):
            tile(q, strip, *STRIPS[strip])
            return carry

        lax.fori_loop(first, last, body, 0)

    s1_send()
    for second in range(2):
        for sign in both:
            z_move(sign, 1, second)
    c_move(0)
    t1_send(0)
    s1_recv()
    z_step(1, 0)
    t1_recv(0)
    z_step(1, 1)
    for sign in both:
        c_move(sign)
    s2_recv()
    z_step(2, 0)
    t1_recv(1)
    z_step(2, 1)
    for sign in both:
        c_move(2 * sign)
    t1_recv(2)
    c_come(0)
    tiles(0, 1, 0)
    z_step(3, 0)
    tiles(1, 2, 0)
    t1_recv(3)
    z_step(3, 1)
    for sign in both:
        c_move(3 * sign)
    tiles(2, 3, 0)
    c_come(1)
    tiles(0, 3, 1)
    z_step(4, 0)
    c_move(4)
    t2_recv()
    tile(3, 0, *LAST[0])
    c_come(2)
    tile(0, 2, *STRIPS[2], count=3)
    tile(3, 1, *LAST[1])

    for part in range(2):
        high = jnp.max(cmax[part], axis=0)
        high = jnp.max(high, axis=0, keepdims=True)
        total = jnp.sum(csum[part] * jnp.exp2(cmax[part] - high[None]), axis=0)
        lse = high + jnp.log2(jnp.sum(total, axis=0, keepdims=True))
        for dz in range(8):
            k = SLOT[dz]
            cst[pl.ds(part * 8 + (z + dz) % 8, 1), :] = lse[:, 128 * k:128 * k + 128]
    for dz, dc in column:
        i, dev = column_peer(dz, dc)
        send(cst, cst_in.at[me_c], cx_s, cx_r, dev)

    for part in range(2):
        for k in range(8):
            rows = pl.ds(128 * k, 128)
            strips = range(3 if k < 6 else 2)
            m = [rmax[part, s, rows, :] for s in strips]
            high = functools.reduce(jnp.maximum, m)
            total = functools.reduce(jnp.add, [rsum[part, s, rows, :] * jnp.exp2(m[s] - high) for s in strips])
            high, total = high.T, total.T
            peak = jnp.max(high, axis=0, keepdims=True)
            lse = peak + jnp.log2(jnp.sum(total * jnp.exp2(high - peak), axis=0, keepdims=True))
            for h, a, b, r in UNITS:
                if r // 128 == k:
                    o = r % 128
                    rel[pl.ds(part * 8 + h * 4 + b, 1), pl.ds(32 * a, 32)] = lse[:, o:o + 32]
        v = rel[pl.ds(part * 8, 8), :]
        v = (pltpu.roll(v, 32 * x, axis=1), pltpu.roll(v, 32 * y, axis=1))
        for h in range(2):
            for b in range(4):
                k = h * 4 + b
                rst[pl.ds(part * 8 + h * 4 + (b + (y, x)[h]) % 4, 1), :] = v[h][k:k + 1]
    for dx, dy in plane:
        i, dev = plane_peer(dx, dy)
        send(rst, rst_in.at[me_p], rx_s, rx_r, dev)
    cst_in[me_c] = cst[...]
    rst_in[me_p] = rst[...]

    def total_lse(v):
        m = jnp.max(v, axis=0)
        return m + jnp.log2(jnp.sum(jnp.exp2(v - m[None]), axis=0))

    half = 0.5 * sscale[0]
    arrived(cst_in.at[pl.ds(0, 15)], cx_s, cx_r)
    col = total_lse(cst_in[...])
    call[...] = col
    for part in range(2):
        lse = [None] * 8
        for dz in range(8):
            lse[SLOT[dz]] = call[pl.ds(part * 8 + (z + dz) % 8, 1), :]
        cmax[part] = half * jnp.exp2(cmax[part] - jnp.concatenate(lse, axis=1)[None])
    arrived(rst_in.at[pl.ds(0, 15)], rx_s, rx_r)
    row = total_lse(rst_in[...])
    rall[...] = row
    for part in range(2):
        for h in range(2):
            for b in range(4):
                rel[pl.ds(part * 8 + h * 4 + b, 1), :] = rall[pl.ds(part * 8 + h * 4 + (b + (y, x)[h]) % 4, 1), :]
        v = rel[pl.ds(part * 8, 8), :]
        v = (pltpu.roll(v, 128 - 32 * x, axis=1), pltpu.roll(v, 128 - 32 * y, axis=1))
        for k in range(8):
            mine = sorted((r, h, a, b) for h, a, b, r in UNITS if r // 128 == k)
            lse = jnp.concatenate(
                [v[h][h * 4 + b:h * 4 + b + 1, 32 * a:32 * a + 32] for _, h, a, b in mine], axis=1
            )
            lse = jnp.broadcast_to(lse, (128, 128)).T
            rows = pl.ds(128 * k, 128)
            for s in range(3 if k < 6 else 2):
                rmax[part, s, rows, :] = half * jnp.exp2(rmax[part, s, rows, :] - lse)

    def pass2(pieces, carry):
        def body(s, carry, group):
            loss_acc, scale_acc = carry
            rows = pl.ds(pl.multiple_of(s * 32, 32), 32)
            q = s // (CHUNK // 32)
            for c0, n, *strips in pieces:
                cols = pl.ds(c0, n)
                k = n // 128
                strip = strips[group]
                v = vs[rows, cols]
                teach = ert[rows, cols] * wide(rmax[0, strip, rows, :], k) + ect[rows, cols] * tall(cmax[0, q, :, cols], 4)
                stud = ers[rows, cols] * wide(rmax[1, strip, rows, :], k) + ecs[rows, cols] * tall(cmax[1, q, :, cols], 4)
                differ = stud - teach
                wts[rows, cols] = differ.astype(jnp.bfloat16)
                loss_acc = loss_acc + lanes(sublanes(teach * v, jnp.add), jnp.add)
                scale_acc = scale_acc + lanes(sublanes(differ * v, jnp.add), jnp.add)
            return loss_acc, scale_acc

        carry = lax.fori_loop(0, 24, functools.partial(body, group=0), carry, unroll=2)
        return lax.fori_loop(24, 32, functools.partial(body, group=1), carry, unroll=2)

    slots = ((5, 3), (3, 2), (1, 2), (0, 1))

    def text_parts(i):
        k, n = slots[i]
        v = lax.dot_general(
            wts[:, 128 * k:128 * (k + n)], img[:, TW:], TN, preferred_element_type=jnp.float32
        )
        some = pl.ds(k, n)
        gt_all[some] = v.reshape(n, 2, ROWS, SW)
        send(gt_all.at[some, sib], gt_sib.at[some], sb_s, sb_r.at[i], other)

    def text_both(i):
        arrived(gt_sib.at[pl.ds(*slots[i])], sb_s, sb_r.at[i])

    def own_part(dz, q):
        rows = pl.ds(32 * q, 32)
        return gt_all[SLOT[dz % 8], c, rows, :] + gt_sib[SLOT[dz % 8], rows, :]

    def chain_ref(ref, sign, s, q):
        return ref.at[s * 2 + (sign > 0), pl.ds(32 * q, 32)]

    def chain_wait(s, second):
        arrived(gt_in.at[0], gt_s, gt_r.at[s * 2 + second])

    def chain_part(sign, s, q):
        return chain_ref(gt_in, sign, s, q)[...].astype(jnp.float32)

    def chain_send(s, second):
        for sign in both:
            q = first_half(sign) ^ second
            v = own_part(sign * (3 - s), q)
            if s > 0:
                v = v + chain_part(sign, s - 1, q)
            if s == 1 and not second:
                v = v + gt_in[6, pl.ds(32 * q, 32), :].astype(jnp.float32)
            chain_ref(gt_snd, sign, s, q)[...] = v.astype(jnp.bfloat16)
            send(chain_ref(gt_snd, sign, s, q), chain_ref(gt_in, sign, s, q), gt_s, gt_r.at[s * 2 + second], up(sign))

    def far_send():
        for sign in both:
            rows = pl.ds(32 * first_half(sign), 32)
            gt_snd[6, rows] = own_part(4, first_half(sign)).astype(jnp.bfloat16)
            send(gt_snd.at[6, rows], gt_in.at[6, rows], gt_s, gt_r.at[6], up(2 * sign))

    def image_parts(q):
        v = jnp.dot(
            wts[pl.ds(256 * q, 256), :], txt[:, :, :, TW:].reshape(TILE, SW), preferred_element_type=jnp.float32
        )
        for h, a, b, r in UNITS:
            if r // 256 == q:
                o = r % 256
                if b == 0:
                    gi_own[h, a] = v[o:o + 32]
                else:
                    gi_snd[h, b, a] = v[o:o + 32].astype(jnp.bfloat16)

    pieces = ((2, 2), (1, 1), (0, 1))

    def stage1_send(b, p):
        for h in range(2):
            part = pl.ds(*pieces[p])
            send(gi_snd.at[h, b, part], gi_in.at[h, 4 - b, part], g1_s, g1_r.at[h * 3 + p], along(h, 1, b))

    def stage1_sum(h, p):
        first_a, count = pieces[p]
        arrived(gi_in.at[h, pl.ds(1, 3), pl.ds(first_a, count)], g1_s, g1_r.at[h * 3 + p])
        for a in range(first_a, first_a + count):
            v = gi_own[h, a] + gi_in[h, 1, a].astype(jnp.float32)
            v = v + gi_in[h, 2, a].astype(jnp.float32) + gi_in[h, 3, a].astype(jnp.float32)
            if a == 0:
                gi_mid[h] = v
            else:
                g2_snd[h, a] = v.astype(jnp.bfloat16)
                send(g2_snd.at[h, a], g2_in.at[h, 4 - a], g2_s, g2_r.at[h], along(h, 0, a))

    def stage2_sum(h):
        arrived(g2_in.at[h, pl.ds(1, 3)], g2_s, g2_r.at[h])
        v = gi_mid[h]
        for a in range(1, 4):
            v = v + g2_in[h, a].astype(jnp.float32)
        out[pl.ds(32 * h, 32), :] = v

    def scalar_send(level, peers, peer, me):
        for p in peers:
            i, dev = peer(*p)
            send(sc_snd.at[level], sc_in.at[level, me], sc_s, sc_r.at[level], dev)

    def scalar_sum(level, me):
        arrived(sc_in.at[level, pl.ds(0, 15)], sc_s, sc_r.at[level])
        sc_in[level, me] = sc_snd[level]
        return jnp.sum(sc_in[level], axis=0)

    in_plane = (plane, plane_peer, me_p)
    in_column = (column, column_peer, me_c)

    zero = jnp.zeros((8, 128), jnp.float32)
    accs = pass2(((640, 128, 1, 1), (768, 256, 2, 1)), (zero, zero))
    text_parts(0)
    loss_acc, scale_acc = pass2(((512, 128, 1, 1), (0, 512, 0, 0)), accs)

    back = LN2 / half
    loss_acc = (row[8:, :] + col[8:, :]) * (LN2 / 16.0) - loss_acc * back
    sc_snd[0, pl.ds(0, 1), :] = jnp.sum(loss_acc, axis=0, keepdims=True)
    sc_snd[0, pl.ds(1, 1), :] = jnp.sum(scale_acc * back, axis=0, keepdims=True)
    scalar_send(0, *in_plane)

    text_both(0)
    far_send()
    chain_send(0, 1)
    chain_send(0, 0)
    text_parts(1)
    for q in (3, 1, 2):
        image_parts(q)
    for p in range(3):
        for b in (2, 1, 3):
            stage1_send(b, p)
    text_parts(2)
    text_both(1)
    chain_wait(0, 1)
    chain_send(1, 1)
    chain_wait(0, 0)
    arrived(gt_in.at[6], gt_s, gt_r.at[6])
    chain_send(1, 0)
    image_parts(0)
    text_parts(3)
    sc_snd[1] = scalar_sum(0, me_p)
    scalar_send(1, *in_column)
    text_both(2)
    chain_wait(1, 1)
    chain_send(2, 1)
    for h in range(2):
        stage1_sum(h, 0)
    chain_wait(1, 0)
    chain_send(2, 0)
    for h in range(2):
        stage1_sum(h, 1)
    for h in range(2):
        stage1_sum(h, 2)
    text_both(3)
    total = scalar_sum(1, me_c)
    for h in range(2):
        stage2_sum(h)
    for second in (1, 0):
        chain_wait(2, second)
    for q in range(2):
        out[pl.ds(ROWS + 32 * q, 32), :] = own_part(0, q) + chain_part(1, 2, q) + chain_part(-1, 2, q)
    pairs = 2.0 * TILE * 16
    out[pl.ds(2 * ROWS, 1), pl.ds(0, 128)] = total[:1] / pairs
    out[pl.ds(2 * ROWS + 1, 1), pl.ds(0, 128)] = total[1:] / (pairs * sscale[0])
    all_sent(img.at[pl.ds(0, 960)], ps_s, ps_r.at[0])
    all_sent(txt.at[pl.ds(0, 7), 0], zs_s, zs_r.at[0])
    all_sent(txt.at[:, 0], cs_s, cs_r.at[0])
    all_sent(rst_in.at[pl.ds(0, 15)], rx_s, rx_r)
    all_sent(cst_in.at[pl.ds(0, 15)], cx_s, cx_r)
    all_sent(gi_in.at[:, pl.ds(0, 3)], g1_s, g1_r.at[0])
    all_sent(g2_in.at[:, pl.ds(0, 3)], g2_s, g2_r.at[0])
    all_sent(gt_sib, sb_s, sb_r.at[0])
    all_sent(gt_in.at[pl.ds(0, 7)], gt_s, gt_r.at[0])
    all_sent(sc_in.at[:, pl.ds(0, 15)], sc_s, sc_r.at[0])


def finish(both, gi_out, gt_out, loss_out, gs_out):
    gi_out[...] = both[pl.ds(0, ROWS), :]
    gt_out[...] = both[pl.ds(ROWS, ROWS), :]
    loss_out[0] = jnp.sum(both[pl.ds(2 * ROWS, 1), pl.ds(0, 128)])
    gs_out[0] = jnp.sum(both[pl.ds(2 * ROWS + 1, 1), pl.ds(0, 128)])


def shards(*args):
    f32, bf16 = jnp.float32, jnp.bfloat16
    anyw = pl.BlockSpec(memory_space=pl.ANY)
    vmem = pl.BlockSpec(memory_space=pltpu.VMEM)
    smem = pl.BlockSpec(memory_space=pltpu.SMEM)
    sem = pltpu.SemaphoreType.DMA
    V = pltpu.VMEM
    rows = jax.ShapeDtypeStruct((ROWS, SW), f32)
    one = jax.ShapeDtypeStruct((1,), f32)
    results = pl.pallas_call(
        kernel,
        out_shape=jax.ShapeDtypeStruct((2 * ROWS + 8, SW), f32),
        in_specs=[anyw] * 4 + [smem] * 2,
        out_specs=vmem,
        scratch_shapes=[
            V((TILE, W), bf16),
            V((NZ, 2, ROWS, W), bf16),
            V((TILE, TILE), f32),
            V((TILE, TILE), f32),
            V((TILE, TILE), f32),
            V((TILE, TILE), f32),
            V((TILE, TILE), f32),
            V((TILE, TILE), f32),
            V((TILE, TILE), bf16),
            V((2, 3, TILE, 128), f32),
            V((2, 3, TILE, 128), f32),
            V((2, 4, 8, TILE), f32),
            V((2, 4, 8, TILE), f32),
            V((16, 128), f32),
            V((16, 128), f32),
            V((16, 128), f32),
            V((16, 128), f32),
            V((16, 128), f32),
            V((16, 16, 128), f32),
            V((16, 16, 128), f32),
            V((2, 4, 32, SW), f32),
            V((2, 32, SW), f32),
            V((2, 4, 4, 32, SW), bf16),
            V((2, 4, 4, 32, SW), bf16),
            V((2, 4, 32, SW), bf16),
            V((2, 4, 32, SW), bf16),
            V((8, 2, ROWS, SW), f32),
            V((8, ROWS, SW), f32),
            V((8, ROWS, SW), bf16),
            V((8, ROWS, SW), bf16),
            V((2, 2, 128), f32),
            V((2, 16, 2, 128), f32),
            sem,
            sem, sem((7,)),
            sem, sem((7,)),
            sem, sem((3,)),
            sem, sem,
            sem, sem,
            sem, sem((6,)),
            sem, sem((2,)),
            sem, sem((4,)),
            sem, sem((7,)),
            sem, sem((2,)),
        ],
        compiler_params=pltpu.CompilerParams(
            collective_id=0, has_side_effects=True, vmem_limit_bytes=60 * 1024 * 1024
        ),
    )(*args)
    return tuple(pl.pallas_call(
        finish,
        out_shape=(rows, rows, one, one),
        in_specs=[vmem],
        out_specs=(vmem, vmem, smem, smem),
    )(results))


def solution(mesh):
    return jax.shard_map(
        shards,
        mesh=mesh,
        in_specs=(
            P(("grp", "dev"), None),
            P(("grp", "dev"), None),
            P(("grp", "dev"), None),
            P(("grp", "dev"), None),
            P(),
            P(),
        ),
        out_specs=(P(("grp", "dev"), None), P(("grp", "dev"), None), P(), P()),
        check_vma=False,
    )
```

```python
import functools

import jax
import jax.numpy as jnp
from jax import lax
from jax.experimental import pallas as pl
from jax.experimental.pallas import tpu as pltpu
from jax.sharding import PartitionSpec as P

NX, NY, NZ = 4, 4, 8
ROWS = 64
TW, SW = 1280, 512
W = TW + SW
TILE = 1024
CHUNK = 256
LOG2E = 1.4426950408889634
LN2 = 0.6931471805599453
MESH = pl.DeviceIdType.MESH
NT = (((1,), (1,)), ((), ()))
TN = (((0,), (0,)), ((), ()))

A_OF = (0, 3, 1, 2)
SLOT = (0, 1, 3, 5, 7, 6, 4, 2)
STRIPS = ((0, 512), (512, 256), (768, 256))
LAST = ((0, 512), (512, 512))


def row_unit(h, a, b):
    k = A_OF.index(a)
    if b == 0:
        return 128 * h + 32 * a
    if b == 2:
        return 768 + 64 * k + 32 * h
    return 256 + 128 * k + (0 if b == 3 else 64) + 32 * h


UNITS = tuple((h, a, b, row_unit(h, a, b)) for h in range(2) for a in range(4) for b in range(4))


def lanes(v, op):
    return functools.reduce(op, [v[:, 128 * k:128 * k + 128] for k in range(v.shape[1] // 128)])


def sublanes(v, op):
    return functools.reduce(op, [v[8 * k:8 * k + 8] for k in range(v.shape[0] // 8)])


def wide(v, n):
    return jnp.concatenate([v] * n, axis=1)


def tall(v, n):
    return jnp.concatenate([v] * n, axis=0)


def kernel(
    ti, tt, si, st, tscale, sscale,
    out,
    img, txt, vt, vs, ert, ect, ers, ecs, wts,
    rmax, rsum, cmax, csum, rel, rst, cst, rall, call, rst_in, cst_in,
    gi_own, gi_mid, gi_snd, gi_in, g2_snd, g2_in, gt_all, gt_sib, gt_snd, gt_in,
    sc_snd, sc_in,
    loc_sem, ps_s, ps_r, zs_s, zs_r, cs_s, cs_r,
    rx_s, rx_r, cx_s, cx_r, g1_s, g1_r, g2_s, g2_r, sb_s, sb_r, gt_s, gt_r,
    sc_s, sc_r,
):
    g, d = lax.axis_index("grp"), lax.axis_index("dev")
    x, y, z, c = g % 4, d // 4, ((d // 2) % 2) * 4 + g // 4, d % 2
    me_p, me_c = y * 4 + x, z * 2 + c
    sib = 1 - c

    def at(xx, yy, zz, cc):
        return ((zz % 4) * 4 + xx, yy * 4 + (zz // 4) * 2 + cc)

    plane = [(dx, dy) for dy in range(NY) for dx in range(NX) if (dx, dy) != (0, 0)]
    column = [(dz, dc) for dz in range(NZ) for dc in range(2) if (dz, dc) != (0, 0)]

    def plane_peer(dx, dy):
        px, py = (x + dx) % NX, (y + dy) % NY
        return py * 4 + px, at(px, py, z, c)

    def column_peer(dz, dc):
        pz, pc = (z + dz) % NZ, (c + dc) % 2
        return pz * 2 + pc, at(x, y, pz, pc)

    def along(h, axis, step):
        if (h + axis) % 2 == 0:
            return at((x + step) % NX, y, z, c)
        return at(x, (y + step) % NY, z, c)

    def up(step):
        return at(x, y, (z + step) % NZ, c)

    other = at(x, y, z, sib)

    local = []

    def bring(src, dst):
        cp = pltpu.make_async_copy(src, dst, loc_sem)
        cp.start()
        local.append(cp)

    for h in range(2):
        r = row_unit(h, 0, 0)
        bring(ti.at[pl.ds(32 * h, 32)], img.at[pl.ds(r, 32), pl.ds(0, TW)])
        bring(si.at[pl.ds(32 * h, 32)], img.at[pl.ds(r, 32), pl.ds(TW, SW)])
    bring(tt, txt.at[0, c, :, pl.ds(0, TW)])
    bring(st, txt.at[0, c, :, pl.ds(TW, SW)])

    barrier = pltpu.get_barrier_semaphore()
    near = [along(0, axis, step) for axis in range(2) for step in (1, -1)] + [up(1), up(-1), other]
    for dev in near:
        pl.semaphore_signal(barrier, inc=1, device_id=dev, device_id_type=MESH)
    pltpu.make_async_copy(img.at[pl.ds(0, 2 * ROWS)], img.at[pl.ds(0, 2 * ROWS)], loc_sem).wait()
    pl.semaphore_wait(barrier, len(near))

    def remote(src, dst, ssem, rsem, dev):
        return pltpu.make_async_remote_copy(
            src_ref=src, dst_ref=dst, send_sem=ssem, recv_sem=rsem, device_id=dev, device_id_type=MESH
        )

    def send(src, dst, ssem, rsem, dev):
        remote(src, dst, ssem, rsem, dev).start()

    def arrived(like, ssem, rsem):
        remote(like, like, ssem, rsem, other).wait_recv()

    def all_sent(like, ssem, rsem):
        remote(like, like, ssem, rsem, other).wait_send()

    both = (1, -1)

    def unit(h, a, b, r0=0, n=32):
        return img.at[pl.ds(row_unit(h, a % 4, b % 4) + r0, n)]

    def psend(h, i, sign, src, dst, axis):
        send(src, dst, ps_s, ps_r.at[i], along(h, axis, sign))

    def pwait(i, n):
        arrived(img.at[pl.ds(0, n)], ps_s, ps_r.at[i])

    def half_of(sign):
        return (0 if sign > 0 else 16), 16

    hs = [(h, sign) for h in range(2) for sign in both]

    def s1_send():
        for h, sign in hs:
            psend(h, 0, sign, unit(h, 0, 0), unit(h, -sign, 0), 0)

    def s1_recv():
        pwait(0, 128)
        for h, sign in hs:
            psend(h, 1, sign, unit(h, -sign, 0, *half_of(sign)), unit(h, 2, 0, *half_of(sign)), 0)
        t1_send(1)
        t1_send(2)

    def s2_recv():
        pwait(1, 64)
        t1_send(3)

    def t1_send(k):
        for h, sign in hs:
            psend(h, 2 + k, sign, unit(h, A_OF[k], 0), unit(h, A_OF[k], -sign), 1)

    def t1_recv(k):
        pwait(2 + k, 128)
        for h, sign in hs:
            psend(h, 6, sign, unit(h, A_OF[k], -sign, *half_of(sign)), unit(h, A_OF[k], 2, *half_of(sign)), 1)

    def t2_recv():
        pwait(6, 256)

    def zpart(dz, q):
        return txt.at[SLOT[dz % 8], c, pl.ds(32 * q, 32)]

    def first_half(sign):
        return 0 if sign > 0 else 1

    def z_move(sign, s, second):
        q = first_half(sign) ^ second
        send(zpart(-sign * (s - 1), q), zpart(-sign * s, q), zs_s, zs_r.at[(s - 1) * 2 + second], up(sign))

    def z_step(s, second):
        arrived(txt.at[0, 0], zs_s, zs_r.at[(s - 1) * 2 + second])
        for sign in both:
            if s < 3 or (s == 3 and not second):
                z_move(sign, s + 1, second)

    groups = ((0, 4), (4, 2), (6, 2))

    def c_move(dz):
        k = SLOT[dz % 8]
        i = (k >= 4) + (k >= 6)
        send(txt.at[k, c], txt.at[k, c], cs_s, cs_r.at[i], other)

    def c_come(i):
        arrived(txt.at[pl.ds(*groups[i]), sib], cs_s, cs_r.at[i])

    lt, ls = tscale[0] * LOG2E, sscale[0] * LOG2E
    parts = ((0, TW, lt, vt, ert, ect), (TW, W, ls, vs, ers, ecs))

    def tile(q, strip, c0, n, count=1):
        cols = pl.ds(c0, n)
        blocks = pl.ds(c0 // 128, n // 128)
        for part, (lo, hi, scale, raw, er, ec) in enumerate(parts):
            all_rows = pl.ds(q * CHUNK, count * CHUNK)
            raw[all_rows, cols] = scale * lax.dot_general(
                img[all_rows, lo:hi],
                txt[blocks, :, :, lo:hi].reshape(n, hi - lo),
                NT,
                preferred_element_type=jnp.float32,
            )
            for g in range(count):
                r0 = (q + g) * CHUNK
                peak = None
                for s in range(CHUNK // 32):
                    rows = pl.ds(r0 + 32 * s, 32)
                    v = raw[rows, cols]
                    m = lanes(v, jnp.maximum)
                    e = jnp.exp2(v - wide(m, n // 128))
                    er[rows, cols] = e
                    rmax[part, strip, rows, :] = m
                    rsum[part, strip, rows, :] = lanes(e, jnp.add)
                    high = sublanes(v, jnp.maximum)
                    peak = high if peak is None else jnp.maximum(peak, high)
                total = None
                for s in range(CHUNK // 32):
                    rows = pl.ds(r0 + 32 * s, 32)
                    e = jnp.exp2(raw[rows, cols] - tall(peak, 4))
                    ec[rows, cols] = e
                    add = sublanes(e, jnp.add)
                    total = add if total is None else total + add
                cmax[part, q + g, :, cols] = peak
                csum[part, q + g, :, cols] = total

    def tiles(first, last, strip):
        def body(q, carry):
            tile(q, strip, *STRIPS[strip])
            return carry

        lax.fori_loop(first, last, body, 0)

    s1_send()
    for second in range(2):
        for sign in both:
            z_move(sign, 1, second)
    c_move(0)
    t1_send(0)
    s1_recv()
    z_step(1, 0)
    t1_recv(0)
    z_step(1, 1)
    for sign in both:
        c_move(sign)
    s2_recv()
    z_step(2, 0)
    t1_recv(1)
    z_step(2, 1)
    for sign in both:
        c_move(2 * sign)
    t1_recv(2)
    c_come(0)
    tiles(0, 1, 0)
    z_step(3, 0)
    tiles(1, 2, 0)
    t1_recv(3)
    z_step(3, 1)
    for sign in both:
        c_move(3 * sign)
    tiles(2, 3, 0)
    c_come(1)
    tiles(0, 3, 1)
    z_step(4, 0)
    c_move(4)
    t2_recv()
    tile(3, 0, *LAST[0])
    c_come(2)
    tile(0, 2, *STRIPS[2], count=3)
    tile(3, 1, *LAST[1])

    for part in range(2):
        high = jnp.max(cmax[part], axis=0)
        high = jnp.max(high, axis=0, keepdims=True)
        total = jnp.sum(csum[part] * jnp.exp2(cmax[part] - high[None]), axis=0)
        lse = high + jnp.log2(jnp.sum(total, axis=0, keepdims=True))
        for dz in range(8):
            k = SLOT[dz]
            cst[pl.ds(part * 8 + (z + dz) % 8, 1), :] = lse[:, 128 * k:128 * k + 128]
    for dz, dc in column:
        i, dev = column_peer(dz, dc)
        send(cst, cst_in.at[me_c], cx_s, cx_r, dev)

    for part in range(2):
        for k in range(8):
            rows = pl.ds(128 * k, 128)
            strips = range(3 if k < 6 else 2)
            m = [rmax[part, s, rows, :] for s in strips]
            high = functools.reduce(jnp.maximum, m)
            total = functools.reduce(jnp.add, [rsum[part, s, rows, :] * jnp.exp2(m[s] - high) for s in strips])
            high, total = high.T, total.T
            peak = jnp.max(high, axis=0, keepdims=True)
            lse = peak + jnp.log2(jnp.sum(total * jnp.exp2(high - peak), axis=0, keepdims=True))
            for h, a, b, r in UNITS:
                if r // 128 == k:
                    o = r % 128
                    rel[pl.ds(part * 8 + h * 4 + b, 1), pl.ds(32 * a, 32)] = lse[:, o:o + 32]
        v = rel[pl.ds(part * 8, 8), :]
        v = (pltpu.roll(v, 32 * x, axis=1), pltpu.roll(v, 32 * y, axis=1))
        for h in range(2):
            for b in range(4):
                k = h * 4 + b
                rst[pl.ds(part * 8 + h * 4 + (b + (y, x)[h]) % 4, 1), :] = v[h][k:k + 1]
    for dx, dy in plane:
        i, dev = plane_peer(dx, dy)
        send(rst, rst_in.at[me_p], rx_s, rx_r, dev)
    cst_in[me_c] = cst[...]
    rst_in[me_p] = rst[...]

    def total_lse(v):
        m = jnp.max(v, axis=0)
        return m + jnp.log2(jnp.sum(jnp.exp2(v - m[None]), axis=0))

    half = 0.5 * sscale[0]
    arrived(cst_in.at[pl.ds(0, 15)], cx_s, cx_r)
    col = total_lse(cst_in[...])
    call[...] = col
    for part in range(2):
        lse = [None] * 8
        for dz in range(8):
            lse[SLOT[dz]] = call[pl.ds(part * 8 + (z + dz) % 8, 1), :]
        cmax[part] = half * jnp.exp2(cmax[part] - jnp.concatenate(lse, axis=1)[None])
    arrived(rst_in.at[pl.ds(0, 15)], rx_s, rx_r)
    row = total_lse(rst_in[...])
    rall[...] = row
    for part in range(2):
        for h in range(2):
            for b in range(4):
                rel[pl.ds(part * 8 + h * 4 + b, 1), :] = rall[pl.ds(part * 8 + h * 4 + (b + (y, x)[h]) % 4, 1), :]
        v = rel[pl.ds(part * 8, 8), :]
        v = (pltpu.roll(v, 128 - 32 * x, axis=1), pltpu.roll(v, 128 - 32 * y, axis=1))
        for k in range(8):
            mine = sorted((r, h, a, b) for h, a, b, r in UNITS if r // 128 == k)
            lse = jnp.concatenate(
                [v[h][h * 4 + b:h * 4 + b + 1, 32 * a:32 * a + 32] for _, h, a, b in mine], axis=1
            )
            lse = jnp.broadcast_to(lse, (128, 128)).T
            rows = pl.ds(128 * k, 128)
            for s in range(3 if k < 6 else 2):
                rmax[part, s, rows, :] = half * jnp.exp2(rmax[part, s, rows, :] - lse)

    def pass2(pieces, carry):
        def body(s, carry, group):
            loss_acc, scale_acc = carry
            rows = pl.ds(pl.multiple_of(s * 32, 32), 32)
            q = s // (CHUNK // 32)
            for c0, n, *strips in pieces:
                cols = pl.ds(c0, n)
                k = n // 128
                strip = strips[group]
                v = vs[rows, cols]
                teach = ert[rows, cols] * wide(rmax[0, strip, rows, :], k) + ect[rows, cols] * tall(cmax[0, q, :, cols], 4)
                stud = ers[rows, cols] * wide(rmax[1, strip, rows, :], k) + ecs[rows, cols] * tall(cmax[1, q, :, cols], 4)
                differ = stud - teach
                wts[rows, cols] = differ.astype(jnp.bfloat16)
                loss_acc = loss_acc + lanes(sublanes(teach * v, jnp.add), jnp.add)
                scale_acc = scale_acc + lanes(sublanes(differ * v, jnp.add), jnp.add)
            return loss_acc, scale_acc

        carry = lax.fori_loop(0, 24, functools.partial(body, group=0), carry, unroll=4)
        return lax.fori_loop(24, 32, functools.partial(body, group=1), carry, unroll=4)

    slots = ((5, 3), (3, 2), (1, 2), (0, 1))

    def text_parts(i):
        k, n = slots[i]
        v = lax.dot_general(
            wts[:, 128 * k:128 * (k + n)], img[:, TW:], TN, preferred_element_type=jnp.float32
        )
        some = pl.ds(k, n)
        gt_all[some] = v.reshape(n, 2, ROWS, SW)
        send(gt_all.at[some, sib], gt_sib.at[some], sb_s, sb_r.at[i], other)

    def text_both(i):
        arrived(gt_sib.at[pl.ds(*slots[i])], sb_s, sb_r.at[i])

    def own_part(dz, q):
        rows = pl.ds(32 * q, 32)
        return gt_all[SLOT[dz % 8], c, rows, :] + gt_sib[SLOT[dz % 8], rows, :]

    def chain_ref(ref, sign, s, q):
        return ref.at[s * 2 + (sign > 0), pl.ds(32 * q, 32)]

    def chain_wait(s, second):
        arrived(gt_in.at[0], gt_s, gt_r.at[s * 2 + second])

    def chain_part(sign, s, q):
        return chain_ref(gt_in, sign, s, q)[...].astype(jnp.float32)

    def chain_send(s, second):
        for sign in both:
            q = first_half(sign) ^ second
            v = own_part(sign * (3 - s), q)
            if s > 0:
                v = v + chain_part(sign, s - 1, q)
            if s == 1 and not second:
                v = v + gt_in[6, pl.ds(32 * q, 32), :].astype(jnp.float32)
            chain_ref(gt_snd, sign, s, q)[...] = v.astype(jnp.bfloat16)
            send(chain_ref(gt_snd, sign, s, q), chain_ref(gt_in, sign, s, q), gt_s, gt_r.at[s * 2 + second], up(sign))

    def far_send():
        for sign in both:
            rows = pl.ds(32 * first_half(sign), 32)
            gt_snd[6, rows] = own_part(4, first_half(sign)).astype(jnp.bfloat16)
            send(gt_snd.at[6, rows], gt_in.at[6, rows], gt_s, gt_r.at[6], up(2 * sign))

    def image_parts(q):
        v = jnp.dot(
            wts[pl.ds(256 * q, 256), :], txt[:, :, :, TW:].reshape(TILE, SW), preferred_element_type=jnp.float32
        )
        for h, a, b, r in UNITS:
            if r // 256 == q:
                o = r % 256
                if b == 0:
                    gi_own[h, a] = v[o:o + 32]
                else:
                    gi_snd[h, b, a] = v[o:o + 32].astype(jnp.bfloat16)

    pieces = ((2, 2), (1, 1), (0, 1))

    def stage1_send(b, p):
        for h in range(2):
            part = pl.ds(*pieces[p])
            send(gi_snd.at[h, b, part], gi_in.at[h, 4 - b, part], g1_s, g1_r.at[h * 3 + p], along(h, 1, b))

    def stage1_sum(h, p):
        first_a, count = pieces[p]
        arrived(gi_in.at[h, pl.ds(1, 3), pl.ds(first_a, count)], g1_s, g1_r.at[h * 3 + p])
        for a in range(first_a, first_a + count):
            v = gi_own[h, a] + gi_in[h, 1, a].astype(jnp.float32)
            v = v + gi_in[h, 2, a].astype(jnp.float32) + gi_in[h, 3, a].astype(jnp.float32)
            if a == 0:
                gi_mid[h] = v
            else:
                g2_snd[h, a] = v.astype(jnp.bfloat16)
                send(g2_snd.at[h, a], g2_in.at[h, 4 - a], g2_s, g2_r.at[h], along(h, 0, a))

    def stage2_sum(h):
        arrived(g2_in.at[h, pl.ds(1, 3)], g2_s, g2_r.at[h])
        v = gi_mid[h]
        for a in range(1, 4):
            v = v + g2_in[h, a].astype(jnp.float32)
        out[pl.ds(32 * h, 32), :] = v

    def scalar_send(level, peers, peer, me):
        for p in peers:
            i, dev = peer(*p)
            send(sc_snd.at[level], sc_in.at[level, me], sc_s, sc_r.at[level], dev)

    def scalar_sum(level, me):
        arrived(sc_in.at[level, pl.ds(0, 15)], sc_s, sc_r.at[level])
        sc_in[level, me] = sc_snd[level]
        return jnp.sum(sc_in[level], axis=0)

    in_plane = (plane, plane_peer, me_p)
    in_column = (column, column_peer, me_c)

    zero = jnp.zeros((8, 128), jnp.float32)
    accs = pass2(((640, 128, 1, 1), (768, 256, 2, 1)), (zero, zero))
    text_parts(0)
    loss_acc, scale_acc = pass2(((512, 128, 1, 1), (0, 512, 0, 0)), accs)

    back = LN2 / half
    loss_acc = (row[8:, :] + col[8:, :]) * (LN2 / 16.0) - loss_acc * back
    sc_snd[0, pl.ds(0, 1), :] = jnp.sum(loss_acc, axis=0, keepdims=True)
    sc_snd[0, pl.ds(1, 1), :] = jnp.sum(scale_acc * back, axis=0, keepdims=True)
    scalar_send(0, *in_plane)

    text_both(0)
    far_send()
    chain_send(0, 1)
    chain_send(0, 0)
    text_parts(1)
    for q in (3, 1, 2):
        image_parts(q)
    for p in range(3):
        for b in (2, 1, 3):
            stage1_send(b, p)
    text_parts(2)
    text_both(1)
    chain_wait(0, 1)
    chain_send(1, 1)
    chain_wait(0, 0)
    arrived(gt_in.at[6], gt_s, gt_r.at[6])
    chain_send(1, 0)
    image_parts(0)
    text_parts(3)
    sc_snd[1] = scalar_sum(0, me_p)
    scalar_send(1, *in_column)
    text_both(2)
    chain_wait(1, 1)
    chain_send(2, 1)
    for h in range(2):
        stage1_sum(h, 0)
    chain_wait(1, 0)
    chain_send(2, 0)
    for h in range(2):
        stage1_sum(h, 1)
    for h in range(2):
        stage1_sum(h, 2)
    text_both(3)
    total = scalar_sum(1, me_c)
    for h in range(2):
        stage2_sum(h)
    for second in (1, 0):
        chain_wait(2, second)
    for q in range(2):
        out[pl.ds(ROWS + 32 * q, 32), :] = own_part(0, q) + chain_part(1, 2, q) + chain_part(-1, 2, q)
    pairs = 2.0 * TILE * 16
    out[pl.ds(2 * ROWS, 1), pl.ds(0, 128)] = total[:1] / pairs
    out[pl.ds(2 * ROWS + 1, 1), pl.ds(0, 128)] = total[1:] / (pairs * sscale[0])
    all_sent(img.at[pl.ds(0, 960)], ps_s, ps_r.at[0])
    all_sent(txt.at[pl.ds(0, 7), 0], zs_s, zs_r.at[0])
    all_sent(txt.at[:, 0], cs_s, cs_r.at[0])
    all_sent(rst_in.at[pl.ds(0, 15)], rx_s, rx_r)
    all_sent(cst_in.at[pl.ds(0, 15)], cx_s, cx_r)
    all_sent(gi_in.at[:, pl.ds(0, 3)], g1_s, g1_r.at[0])
    all_sent(g2_in.at[:, pl.ds(0, 3)], g2_s, g2_r.at[0])
    all_sent(gt_sib, sb_s, sb_r.at[0])
    all_sent(gt_in.at[pl.ds(0, 7)], gt_s, gt_r.at[0])
    all_sent(sc_in.at[:, pl.ds(0, 15)], sc_s, sc_r.at[0])


def finish(both, gi_out, gt_out, loss_out, gs_out):
    gi_out[...] = both[pl.ds(0, ROWS), :]
    gt_out[...] = both[pl.ds(ROWS, ROWS), :]
    loss_out[0] = jnp.sum(both[pl.ds(2 * ROWS, 1), pl.ds(0, 128)])
    gs_out[0] = jnp.sum(both[pl.ds(2 * ROWS + 1, 1), pl.ds(0, 128)])


def shards(*args):
    f32, bf16 = jnp.float32, jnp.bfloat16
    anyw = pl.BlockSpec(memory_space=pl.ANY)
    vmem = pl.BlockSpec(memory_space=pltpu.VMEM)
    smem = pl.BlockSpec(memory_space=pltpu.SMEM)
    sem = pltpu.SemaphoreType.DMA
    V = pltpu.VMEM
    rows = jax.ShapeDtypeStruct((ROWS, SW), f32)
    one = jax.ShapeDtypeStruct((1,), f32)
    results = pl.pallas_call(
        kernel,
        out_shape=jax.ShapeDtypeStruct((2 * ROWS + 8, SW), f32),
        in_specs=[anyw] * 4 + [smem] * 2,
        out_specs=vmem,
        scratch_shapes=[
            V((TILE, W), bf16),
            V((NZ, 2, ROWS, W), bf16),
            V((TILE, TILE), f32),
            V((TILE, TILE), f32),
            V((TILE, TILE), f32),
            V((TILE, TILE), f32),
            V((TILE, TILE), f32),
            V((TILE, TILE), f32),
            V((TILE, TILE), bf16),
            V((2, 3, TILE, 128), f32),
            V((2, 3, TILE, 128), f32),
            V((2, 4, 8, TILE), f32),
            V((2, 4, 8, TILE), f32),
            V((16, 128), f32),
            V((16, 128), f32),
            V((16, 128), f32),
            V((16, 128), f32),
            V((16, 128), f32),
            V((16, 16, 128), f32),
            V((16, 16, 128), f32),
            V((2, 4, 32, SW), f32),
            V((2, 32, SW), f32),
            V((2, 4, 4, 32, SW), bf16),
            V((2, 4, 4, 32, SW), bf16),
            V((2, 4, 32, SW), bf16),
            V((2, 4, 32, SW), bf16),
            V((8, 2, ROWS, SW), f32),
            V((8, ROWS, SW), f32),
            V((8, ROWS, SW), bf16),
            V((8, ROWS, SW), bf16),
            V((2, 2, 128), f32),
            V((2, 16, 2, 128), f32),
            sem,
            sem, sem((7,)),
            sem, sem((7,)),
            sem, sem((3,)),
            sem, sem,
            sem, sem,
            sem, sem((6,)),
            sem, sem((2,)),
            sem, sem((4,)),
            sem, sem((7,)),
            sem, sem((2,)),
        ],
        compiler_params=pltpu.CompilerParams(
            collective_id=0, has_side_effects=True, vmem_limit_bytes=60 * 1024 * 1024
        ),
    )(*args)
    return tuple(pl.pallas_call(
        finish,
        out_shape=(rows, rows, one, one),
        in_specs=[vmem],
        out_specs=(vmem, vmem, smem, smem),
    )(results))


def solution(mesh):
    return jax.shard_map(
        shards,
        mesh=mesh,
        in_specs=(
            P(("grp", "dev"), None),
            P(("grp", "dev"), None),
            P(("grp", "dev"), None),
            P(("grp", "dev"), None),
            P(),
            P(),
        ),
        out_specs=(P(("grp", "dev"), None), P(("grp", "dev"), None), P(), P()),
        check_vma=False,
    )
```
